32 devices in a mesh: rep: 8 (over z, y), slab: 4 (over x, core).
Axes of the slice: x: 2, y: 2, z: 4, core: 2. Of those that a mesh axis runs over, the one named last changes fastest.
Arguments:
- replica_field: float32 [16, 64, 128, 128], P('rep', 'slab')
- momentum: float32 [16, 64, 128, 128], P('rep', 'slab'), may hold values from -5 to 5
- parent: int32 [16], replicated, may hold values from 0 to 15, as said below
Outputs:
- field_out: float32 [16, 64, 128, 128], P('rep', 'slab')
- momentum_out: float32 [16, 64, 128, 128], P('rep', 'slab')
- action_density: float32 [16], P('rep')
The draws below stay inside these ranges and needn't reach their ends.
Inputs may be any that keep to these rules, and one draw needn't show every extreme that they name: `parent`: exactly 4 entries differ from their own index, at most one among each aligned block of 2 entries; every entry that differs names an index whose own entry equals it.
All inputs are finite; a program needn't handle non-finite values.
Results may differ from the reference program's by a relative error of at most 0.00002.
Values sent between devices are 32-bit elements; how exact they have to be, the bound alone decides.
A program may use at most 128 MiB of HBM per device.

```python
import jax
import jax.numpy as jnp

LX = 128
LY = 128
REP_DEV = 2
NZ = 64
REPLICAS = 16
MIG = 4


def draw_replica_field(key, part):
    key = jax.random.fold_in(key, 3)
    depth = jnp.arange(NZ, dtype=jnp.float32) / NZ
    amplitude = 0.6 + 1.2 * depth
    values = jnp.clip(jax.random.normal(key, (REPLICAS, NZ, LX, LY), jnp.float32), -4.0, 4.0)
    return (values * amplitude[None, :, None, None]).astype(jnp.float32)


def draw_parent(key, part):
    key = jax.random.fold_in(key, 11)
    keys = jax.random.split(key, 5)
    groups = REPLICAS // REP_DEV
    order = jax.random.permutation(keys[0], groups).astype(jnp.int32)
    dropped_groups = order[:MIG]
    donor_groups = order[MIG:]
    dropped_local = jax.random.randint(keys[1], (MIG,), 0, REP_DEV).astype(jnp.int32)
    first_pick = jax.random.randint(keys[2], (MIG,), 0, groups - MIG)
    second_pick = jax.random.randint(keys[3], (MIG,), 0, groups - MIG)
    picked = jnp.minimum(first_pick, second_pick).astype(jnp.int32)
    donor_local = jax.random.randint(keys[4], (MIG,), 0, REP_DEV).astype(jnp.int32)
    slots = dropped_groups * REP_DEV + dropped_local
    sources = donor_groups[picked] * REP_DEV + donor_local
    parents = jnp.arange(REPLICAS, dtype=jnp.int32)
    return parents.at[slots].set(sources).astype(jnp.int32)


def shard_levels(key, extent, cuts, low, high):
    def one(position, parts):
        heights = jax.random.uniform(jax.random.fold_in(jax.random.fold_in(key, 6), position), (parts,), jnp.float32, low / len(cuts), high / len(cuts))
        return jnp.repeat(jnp.exp(heights), extent[position] // parts).reshape((-1,) + (1,) * (len(extent) - position - 1))

    gain = one(*cuts[0])
    for cut in cuts[1:]:
        gain = gain * one(*cut)
    return gain


def normal_values(rng, extent, scale, limit, pieces=(), held_as=jnp.bfloat16):
    level = shard_levels(rng, extent, pieces, -0.22, 0.18) if pieces else 1.0
    entries = jax.random.normal(rng, extent, jnp.float32) * scale * level
    return jnp.minimum(jnp.maximum(entries, -limit), limit).astype(held_as)


def setup_inputs(seed: int = 0) -> dict:
    splits = jax.random.split(jax.random.key(seed), 4)
    return {
        "replica_field": draw_replica_field(jax.random.fold_in(splits[3], 71), 0),
        "momentum": normal_values(splits[1], (REPLICAS, NZ, LX, LY), 1.0, 5.0, ((0, 8), (1, 4)), jnp.float32),
        "parent": draw_parent(jax.random.fold_in(splits[3], 71), 0),
    }


coupling = 0.5
mass_square = -1.0
step_size = 0.15


def force_of(values):
    nearby = jnp.roll(values, 1, 1) + jnp.roll(values, -1, 1)
    nearby = nearby + jnp.roll(values, 1, 2) + jnp.roll(values, -1, 2)
    nearby = nearby + jnp.roll(values, 1, 3) + jnp.roll(values, -1, 3)
    return nearby - 6.0 * values - mass_square * values - coupling * values * values * values


def action_of(values):
    along_z = jnp.roll(values, -1, 1) - values
    along_x = jnp.roll(values, -1, 2) - values
    along_y = jnp.roll(values, -1, 3) - values
    local = 0.5 * (along_z * along_z + along_x * along_x + along_y * along_y)
    local = local + 0.5 * mass_square * values * values + 0.25 * coupling * values * values * values * values
    return jnp.sum(local, axis=(1, 2, 3)) / (NZ * LX * LY)


def reference(replica_field, momentum, parent):
    start = jnp.take(replica_field, parent.astype(jnp.int32), axis=0)
    density = action_of(start)
    half_kick = momentum + (0.5 * step_size) * force_of(start)
    field_mid = start + step_size * half_kick
    kicked = half_kick + step_size * force_of(field_mid)
    field_end = field_mid + step_size * kicked
    momentum_end = kicked + (0.5 * step_size) * force_of(field_end)
    return field_end, momentum_end, density
```

```python
import functools

import jax
import jax.numpy as jnp
from jax import lax
from jax.experimental import pallas as pl
from jax.experimental.pallas import tpu as pltpu
from jax.sharding import PartitionSpec as P

coupling = 0.5
mass_square = -1.0
step_size = 0.15

ROWS = 4
SPLIT = 2


def holder_row(replica):
    return replica // 4


def links_needed(parent):
    pair = parent.reshape(2 * ROWS, 2)
    own = jnp.arange(4 * ROWS, dtype=jnp.int32).reshape(2 * ROWS, 2)
    wanted = jnp.max(jnp.where(pair != own, pair, -1), axis=1).reshape(ROWS, 2)
    names = jnp.arange(4 * ROWS, dtype=jnp.int32)
    side = (names // 2) % 2
    column = jnp.arange(2, dtype=jnp.int32)
    across = jnp.any(wanted[None] == names[:, None, None], axis=1) & (side[:, None] != column[None])
    most = jnp.max(jnp.sum(across.reshape(ROWS, 2, 2, 2).astype(jnp.int32), axis=2))
    place = jnp.arange(ROWS, dtype=jnp.int32)
    same = wanted[:, None] == wanted[None]
    above = jnp.any(same & (place[None, :, None] > place[:, None, None]), axis=1)
    below = jnp.any(same & (place[None, :, None] < place[:, None, None]), axis=1)
    row = holder_row(wanted)
    at = place[:, None, None]
    dest = place[None, :, None]
    valid = (wanted >= 0)[None]
    up = valid & (dest > at) & (row[None] <= at) & ~above[None]
    down = valid & (dest < at) & (row[None] >= at) & ~below[None]
    most = jnp.maximum(most, jnp.max(jnp.sum(up.astype(jnp.int32), axis=1)))
    return jnp.maximum(most, jnp.max(jnp.sum(down.astype(jnp.int32), axis=1)))


def as_int(flag):
    return jnp.where(flag, 1, 0).astype(jnp.int32)


def line_items(wanted, at, passes, upward):
    items = [jnp.int32(-1)] * passes
    order = range(ROWS - 1, -1, -1) if upward else range(ROWS)
    seen, count = [], jnp.int32(0)
    for dest in order:
        name = wanted[dest]
        row = holder_row(name)
        active = as_int(name >= 0)
        if upward:
            active = active * as_int(dest > at) * as_int(row <= at)
        else:
            active = active * as_int(dest < at) * as_int(row >= at)
        for other in seen:
            active = active * as_int(other != name)
        for p in range(passes):
            items[p] = jnp.where(active * as_int(count == p) == 1, name, items[p])
        count = count + active
        seen.append(name)
    return items


def cross_items(wanted, first, passes):
    need = []
    for local in range(2):
        flag = jnp.int32(0)
        for dest in range(ROWS):
            flag = jnp.maximum(flag, as_int(wanted[dest] == first + local))
        need.append(flag)
    items = [jnp.where(need[0] == 1, first, jnp.where(need[1] == 1, first + 1, -1))]
    if passes > 1:
        items.append(jnp.where(need[0] * need[1] == 1, first + 1, -1))
    return items


def pick(name, candidates):
    value = candidates[0][1]
    for other, block in candidates[1:]:
        value = jnp.where(other == name, block, value)
    return value


def force(lower, center, upper):
    top = pltpu.roll(center, center.shape[0] - 1, 0)
    bottom = pltpu.roll(center, 1, 0)
    right = pltpu.roll(center, center.shape[1] - 1, 1)
    left = pltpu.roll(center, 1, 1)
    nearby = (lower + upper) + (top + bottom) + (right + left)
    value = nearby - center * ((6.0 + mass_square) + coupling * (center * center))
    return value, top, right


def kernel(passes, slabs, delay, volume,
           parent_ref, field_ref, mom_ref, out_f, out_m, out_a,
           own, moved, mom, kick, mid, kick_b, end, rest_f, rest_m, sums, tiles, tiles_in,
           y_out, y_in, up_out, up_in, dn_out, dn_in,
           load_sem, halo_s, halo_r, y_s, y_r, up_s, up_r, dn_s, dn_r, act_s, act_r):
    depth, wx, wy = field_ref.shape[1:]
    chunks = depth * SPLIT
    part = wx // SPLIT
    cross = min(passes, 2)
    rep = lax.axis_index("rep")
    slab = lax.axis_index("slab")
    z = rep // 2
    y = rep % 2
    partner = rep + 1 - 2 * y
    above = lax.rem(slab + 1, slabs)
    below = lax.rem(slab + slabs - 1, slabs)

    loads = [
        pltpu.make_async_copy(field_ref, own.at[:, 3:3 + depth], load_sem.at[0]),
        pltpu.make_async_copy(mom_ref, mom.at[:, 2:2 + depth], load_sem.at[1]),
    ]
    for copy in loads:
        copy.start()

    barrier = pltpu.get_barrier_semaphore()

    def greet(device):
        pl.semaphore_signal(barrier, inc=1, device_id=device, device_id_type=pl.DeviceIdType.MESH)

    for far in range(1, slabs):
        greet((rep, lax.rem(slab + far, slabs)))
    greet((partner, slab))

    @pl.when(z > 0)
    def _():
        greet((rep - 2, slab))

    @pl.when(z < ROWS - 1)
    def _():
        greet((rep + 2, slab))

    pl.semaphore_wait(barrier, slabs + as_int(z > 0) + as_int(z < ROWS - 1))

    def remote(src, dst, send, recv, device):
        return pltpu.make_async_remote_copy(
            src_ref=src, dst_ref=dst, send_sem=send, recv_sem=recv,
            device_id=device, device_id_type=pl.DeviceIdType.MESH)

    halos = [
        remote(field_ref.at[:, depth - 3:depth], own.at[:, 0:3], halo_s.at[0], halo_r.at[0], (rep, above)),
        remote(field_ref.at[:, 0:3], own.at[:, depth + 3:depth + 6], halo_s.at[1], halo_r.at[1], (rep, below)),
        remote(mom_ref.at[:, depth - 2:depth], mom.at[:, 0:2], halo_s.at[2], halo_r.at[2], (rep, above)),
        remote(mom_ref.at[:, 0:2], mom.at[:, depth + 2:depth + 4], halo_s.at[3], halo_r.at[3], (rep, below)),
    ]
    for copy in halos:
        copy.start()
    moved_halos = [
        remote(moved.at[depth:depth + 3], moved.at[0:3], halo_s.at[4], halo_r.at[4], (rep, above)),
        remote(moved.at[3:6], moved.at[depth + 3:depth + 6], halo_s.at[5], halo_r.at[5], (rep, below)),
    ]

    by_group = []
    slots = []
    for group in range(2 * ROWS):
        first, second = parent_ref[2 * group], parent_ref[2 * group + 1]
        by_group.append(jnp.where(first != 2 * group, first, jnp.where(second != 2 * group + 1, second, -1)))
        slots.append(as_int(second != 2 * group + 1))
    mine, other = [], []
    for row in range(ROWS):
        mine.append(jnp.where(y == 0, by_group[2 * row], by_group[2 * row + 1]))
        other.append(jnp.where(y == 0, by_group[2 * row + 1], by_group[2 * row]))
    here, slot = jnp.int32(-1), jnp.int32(0)
    for group in range(2 * ROWS):
        here = jnp.where(rep == group, by_group[group], here)
        slot = jnp.where(rep == group, slots[group], slot)
    here = jnp.where(here >= 0, here, 2 * rep)
    y_out_items = cross_items(other, 2 * rep, cross)
    y_in_items = cross_items(mine, 2 * partner, cross)
    up_out_items = line_items(mine, z, passes, True)
    up_in_items = line_items(mine, z - 1, passes, True)
    dn_out_items = line_items(mine, z, passes, False)
    dn_in_items = line_items(mine, z + 1, passes, False)

    def copy_y(c):
        return remote(y_out.at[c], y_in.at[c], y_s.at[c], y_r.at[c], (partner, slab))

    def copy_up(c):
        return remote(up_out.at[c], up_in.at[c], up_s.at[c], up_r.at[c], (rep + 2, slab))

    def copy_dn(c):
        return remote(dn_out.at[c], dn_in.at[c], dn_s.at[c], dn_r.at[c], (rep - 2, slab))

    def layer_of(c):
        k = c // SPLIT
        return jnp.where(k < 3, k, jnp.where(k < 6, k + depth - 6, k - 3))

    def rows_of(c):
        return pl.ds(pl.multiple_of((c % SPLIT) * part, part), part)

    def own_blocks(c):
        layer, rows = layer_of(c), rows_of(c)
        return [(2 * rep, own[0, 3 + layer, rows]), (2 * rep + 1, own[1, 3 + layer, rows])]

    def cross_blocks(c):
        return [(y_in_items[q], y_in[c, q]) for q in range(cross)]

    def up_blocks(c):
        return [(up_in_items[q], up_in[c, q]) for q in range(passes)]

    def dn_blocks(c):
        return [(dn_in_items[q], dn_in[c, q]) for q in range(passes)]

    def layer_step(k, field_at, mom_at, which, emit):
        center = field_at(k)
        upper = field_at(k + 1)
        value, top, right = force(field_at(k - 1), center, upper)
        first = mom_at(k - 1) + (0.5 * step_size) * value
        kick[k] = first
        mid[k] = center + step_size * first

        @pl.when((k >= 3) & (k < depth + 3))
        def _():
            dz, dx, dy = upper - center, top - center, right - center
            square = center * center
            local = 0.5 * (dz * dz + dx * dx + dy * dy)
            local = local + square * (0.5 * mass_square + (0.25 * coupling) * square)
            sums[which] += jnp.sum(local.reshape(wx // 8, 8, wy), axis=0)

        @pl.when(k >= 3)
        def _():
            at = mid[k - 1]
            value, _, _ = force(mid[k - 2], at, mid[k])
            second = kick[k - 1] + step_size * value
            kick_b[k - 1] = second
            end[k - 1] = at + step_size * second

        @pl.when(k >= 5)
        def _():
            at = end[k - 2]
            value, _, _ = force(end[k - 3], at, end[k - 1])
            emit(k - 5, at, kick_b[k - 2] + (0.5 * step_size) * value)

    sums[...] = jnp.zeros_like(sums)
    loads[0].wait()
    loads[1].wait()
    rest = 1 - slot
    steps = depth + 4
    total = chunks + ROWS * delay
    begin_rest = total - steps
    up_skew = delay * (z + 1)
    dn_skew = delay * (ROWS - z)
    end_skew = jnp.maximum(up_skew, dn_skew)

    def rest_emit(layer, field, momentum):
        rest_f[layer] = field
        rest_m[layer] = momentum

    def during(t, skew):
        return (t >= skew) & (t < skew + chunks)

    def step(t, _):
        @pl.when(t < chunks)
        def _():
            blocks = own_blocks(t)
            for p in range(cross):
                y_out[t, p] = pick(y_out_items[p], blocks)
            copy_y(t).start()

        @pl.when(during(t, delay))
        def _():
            copy_y(t - delay).wait_recv()

        @pl.when(during(t, up_skew) & (z > 0))
        def _():
            copy_up(t - up_skew).wait_recv()

        @pl.when(during(t, dn_skew) & (z < ROWS - 1))
        def _():
            copy_dn(t - dn_skew).wait_recv()

        @pl.when(during(t, up_skew) & (z < ROWS - 1))
        def _():
            c = t - up_skew
            blocks = own_blocks(c) + cross_blocks(c) + up_blocks(c)
            for p in range(passes):
                up_out[c, p] = pick(up_out_items[p], blocks)
            copy_up(c).start()

        @pl.when(during(t, dn_skew) & (z > 0))
        def _():
            c = t - dn_skew
            blocks = own_blocks(c) + cross_blocks(c) + dn_blocks(c)
            for p in range(passes):
                dn_out[c, p] = pick(dn_out_items[p], blocks)
            copy_dn(c).start()

        @pl.when(during(t, end_skew))
        def _():
            c = t - end_skew
            blocks = own_blocks(c) + cross_blocks(c) + up_blocks(c) + dn_blocks(c)
            moved[3 + layer_of(c), rows_of(c)] = pick(here, blocks)

        @pl.when(t == end_skew + 6 * SPLIT - 1)
        def _():
            for copy in moved_halos:
                copy.start()

        @pl.when(t == begin_rest)
        def _():
            for copy in halos:
                copy.wait_recv()

        @pl.when(t >= begin_rest)
        def _():
            layer_step(t - begin_rest + 1, lambda k: own[rest, k], lambda k: mom[rest, k], 0, rest_emit)

        return 0

    lax.fori_loop(0, total, step, 0)
    for copy in moved_halos:
        copy.wait_recv()

    def moved_emit(layer, field, momentum):
        other_f, other_m = rest_f[layer], rest_m[layer]
        out_f[0, layer] = jnp.where(slot == 0, field, other_f)
        out_f[1, layer] = jnp.where(slot == 0, other_f, field)
        out_m[0, layer] = jnp.where(slot == 0, momentum, other_m)
        out_m[1, layer] = jnp.where(slot == 0, other_m, momentum)

    def moved_step(k, _):
        layer_step(k, lambda i: moved[i], lambda i: mom[slot, i], 1, moved_emit)
        return 0

    lax.fori_loop(1, steps + 1, moved_step, 0)

    tiles[0] = jnp.where(slot == 0, sums[1], sums[0])
    tiles[1] = jnp.where(slot == 0, sums[0], sums[1])
    shares = [
        remote(tiles, tiles_in.at[far - 1], act_s.at[far - 1], act_r.at[far - 1],
               (rep, lax.rem(slab + far, slabs)))
        for far in range(1, slabs)
    ]
    for copy in shares:
        copy.start()

    for copy in halos + moved_halos:
        copy.wait_send()

    def drain(c, _):
        copy_y(c).wait_send()

        @pl.when(z < ROWS - 1)
        def _():
            copy_up(c).wait_send()

        @pl.when(z > 0)
        def _():
            copy_dn(c).wait_send()

        return 0

    lax.fori_loop(0, chunks, drain, 0)
    for copy in shares:
        copy.wait()
    whole = tiles[...]
    for far in range(1, slabs):
        whole = whole + tiles_in[far - 1]
    out_a[0] = jnp.sum(whole[0]) * (1.0 / volume)
    out_a[1] = jnp.sum(whole[1]) * (1.0 / volume)


def run(passes, slabs, delay, replica_field, momentum, parent):
    pair, depth, wx, wy = replica_field.shape
    chunks = depth * SPLIT
    part = wx // SPLIT
    cross = min(passes, 2)
    f32 = jnp.float32

    def plane(*lead):
        return pltpu.VMEM((*lead, wx, wy), f32)

    def block(count):
        return pltpu.VMEM((chunks, count, part, wy), f32)

    dma = pltpu.SemaphoreType.DMA
    volume = depth * slabs * wx * wy
    return pl.pallas_call(
        functools.partial(kernel, passes, slabs, delay, volume),
        out_shape=(
            jax.ShapeDtypeStruct(replica_field.shape, f32),
            jax.ShapeDtypeStruct(replica_field.shape, f32),
            jax.ShapeDtypeStruct((pair,), f32),
        ),
        in_specs=[
            pl.BlockSpec(memory_space=pltpu.SMEM),
            pl.BlockSpec(memory_space=pl.ANY),
            pl.BlockSpec(memory_space=pl.ANY),
        ],
        out_specs=(
            pl.BlockSpec(memory_space=pltpu.VMEM),
            pl.BlockSpec(memory_space=pltpu.VMEM),
            pl.BlockSpec(memory_space=pltpu.SMEM),
        ),
        scratch_shapes=[
            plane(pair, depth + 6), plane(depth + 6), plane(pair, depth + 4),
            plane(depth + 6), plane(depth + 6), plane(depth + 6), plane(depth + 6),
            plane(depth), plane(depth),
            pltpu.VMEM((2, 8, wy), f32), pltpu.VMEM((2, 8, wy), f32), pltpu.VMEM((slabs - 1, 2, 8, wy), f32),
            block(cross), block(cross), block(passes), block(passes), block(passes), block(passes),
            dma((2,)), dma((6,)), dma((6,)),
            dma((chunks,)), dma((chunks,)), dma((chunks,)), dma((chunks,)), dma((chunks,)), dma((chunks,)),
            dma((slabs - 1,)), dma((slabs - 1,)),
        ],
        compiler_params=pltpu.CompilerParams(
            collective_id=passes, has_side_effects=True, vmem_limit_bytes=56 * 2**20),
    )(parent, replica_field, momentum)


def routed(replica_field, momentum, parent):
    slabs = lax.axis_size("slab")
    branches = [functools.partial(run, passes, slabs, delay) for passes, delay in ((1, 3), (2, 2), (3, 2))]
    return lax.switch(links_needed(parent) - 1, branches, replica_field, momentum, parent)


def padded(shard, sides, width):
    for axis, dim in sides:
        devices, length = (lax.axis_size(axis), shard.shape[dim])
        up = [(i, (i + 1) % devices) for i in range(devices)]
        down = [(j, i) for i, j in up]
        last = lax.slice_in_dim(shard, length - width, length, axis=dim)
        initial = lax.slice_in_dim(shard, 0, width, axis=dim)
        before = lax.ppermute(last, axis, up)
        after = lax.ppermute(initial, axis, down)
        shard = jnp.concatenate([before, shard, after], axis=dim)
    return shard


def force_inner(extended):
    center = extended[:, 1:-1]
    nearby = extended[:, :-2] + extended[:, 2:]
    nearby = nearby + jnp.roll(center, 1, 2) + jnp.roll(center, -1, 2)
    nearby = nearby + jnp.roll(center, 1, 3) + jnp.roll(center, -1, 3)
    return nearby - 6.0 * center - mass_square * center - coupling * center * center * center


def action_inner(extended):
    center = extended[:, 1:-1]
    along_z = extended[:, 2:] - center
    along_x = jnp.roll(center, -1, 2) - center
    along_y = jnp.roll(center, -1, 3) - center
    local = 0.5 * (along_z * along_z + along_x * along_x + along_y * along_y)
    local = (
        local
        + 0.5 * mass_square * center * center
        + 0.25 * coupling * center * center * center * center
    )
    return jnp.sum(local, axis=(1, 2, 3))


def extend_one(values):
    return padded(values, (("slab", 1),), 1)


def shards(replica_field, momentum, parent):
    per_group = replica_field.shape[0]
    depth = replica_field.shape[1]
    width_x = replica_field.shape[2]
    width_y = replica_field.shape[3]
    flat = replica_field.reshape(per_group, depth, width_x * width_y)
    spread = lax.all_to_all(flat, "rep", split_axis=2, concat_axis=0, tiled=True)
    copied = jnp.take(spread, parent, axis=0)
    returned = lax.all_to_all(copied, "rep", split_axis=0, concat_axis=2, tiled=True)
    field_start = returned.reshape(per_group, depth, width_x, width_y)
    volume = depth * lax.axis_size("slab") * width_x * width_y
    extended = extend_one(field_start)
    partial_action = action_inner(extended)
    half_kick = momentum + 0.5 * step_size * force_inner(extended)
    field_mid = field_start + step_size * half_kick
    kicked = half_kick + step_size * force_inner(extend_one(field_mid))
    field_end = field_mid + step_size * kicked
    momentum_end = kicked + 0.5 * step_size * force_inner(extend_one(field_end))
    density = lax.psum(partial_action, "slab") / volume
    return (field_end, momentum_end, density)


def solution(mesh):
    in_specs = (P("rep", "slab", None, None), P("rep", "slab", None, None), P())
    out_specs = (P("rep", "slab", None, None), P("rep", "slab", None, None), P("rep"))
    plan = routed if mesh.shape["rep"] == 2 * ROWS and mesh.shape["slab"] > 2 else shards
    return jax.shard_map(plan, mesh=mesh, in_specs=in_specs, out_specs=out_specs, check_vma=False)
```

```python
import functools

import jax
import jax.numpy as jnp
from jax import lax
from jax.experimental import pallas as pl
from jax.experimental.pallas import tpu as pltpu
from jax.sharding import PartitionSpec as P

coupling = 0.5
mass_square = -1.0
step_size = 0.15

ROWS = 4
SPLIT = 2


def holder_row(replica):
    return replica // 4


def as_int(flag):
    return jnp.where(flag, 1, 0).astype(jnp.int32)


def line_items(wanted, at, passes, upward):
    items = [jnp.int32(-1)] * passes
    order = range(ROWS - 1, -1, -1) if upward else range(ROWS)
    seen, count = [], jnp.int32(0)
    for dest in order:
        name = wanted[dest]
        row = holder_row(name)
        active = as_int(name >= 0)
        if upward:
            active = active * as_int(dest > at) * as_int(row <= at)
        else:
            active = active * as_int(dest < at) * as_int(row >= at)
        for other in seen:
            active = active * as_int(other != name)
        for p in range(passes):
            items[p] = jnp.where(active * as_int(count == p) == 1, name, items[p])
        count = count + active
        seen.append(name)
    return items


def cross_items(wanted, first, passes):
    need = []
    for local in range(2):
        flag = jnp.int32(0)
        for dest in range(ROWS):
            flag = jnp.maximum(flag, as_int(wanted[dest] == first + local))
        need.append(flag)
    items = [jnp.where(need[0] == 1, first, jnp.where(need[1] == 1, first + 1, -1))]
    if passes > 1:
        items.append(jnp.where(need[0] * need[1] == 1, first + 1, -1))
    return items


def wishes(parent_ref):
    names, slots = [], []
    for group in range(2 * ROWS):
        first, second = parent_ref[2 * group], parent_ref[2 * group + 1]
        names.append(jnp.where(first != 2 * group, first, jnp.where(second != 2 * group + 1, second, -1)))
        slots.append(as_int(second != 2 * group + 1))
    return names, slots


def plan_kernel(parent_ref, out_ref):
    names, _ = wishes(parent_ref)
    most = jnp.int32(1)
    for column in range(2):
        wanted = [names[2 * row + column] for row in range(ROWS)]
        for row in range(ROWS):
            carried = [cross_items(wanted, jnp.int32(4 * row + 2 - 2 * column), 2)]
            carried += [line_items(wanted, row, ROWS - 1, upward) for upward in (True, False)]
            for items in carried:
                for p, item in enumerate(items):
                    most = jnp.where(item >= 0, jnp.maximum(most, p + 1), most)
    out_ref[0] = most


def links_needed(parent):
    smem = pl.BlockSpec(memory_space=pltpu.SMEM)
    return pl.pallas_call(
        plan_kernel, out_shape=jax.ShapeDtypeStruct((1,), jnp.int32), in_specs=[smem], out_specs=smem)(parent)[0]


def pick(name, candidates):
    value = candidates[0][1]
    for other, block in candidates[1:]:
        value = jnp.where(other == name, block, value)
    return value


def force(lower, center, upper):
    top = pltpu.roll(center, center.shape[0] - 1, 0)
    bottom = pltpu.roll(center, 1, 0)
    right = pltpu.roll(center, center.shape[1] - 1, 1)
    left = pltpu.roll(center, 1, 1)
    nearby = (lower + upper) + (top + bottom) + (right + left)
    value = nearby - center * ((6.0 + mass_square) + coupling * (center * center))
    return value, top, right


def kernel(passes, slabs, delay, volume,
           parent_ref, field_ref, mom_ref, out_f, out_m, out_a,
           own, moved, mom, kick, mid, kick_b, end, rest_f, rest_m, sums, tiles, tiles_in,
           y_out, y_in, up_out, up_in, dn_out, dn_in,
           load_sem, halo_s, halo_r, y_s, y_r, up_s, up_r, dn_s, dn_r, act_s, act_r):
    depth, wx, wy = field_ref.shape[1:]
    chunks = depth * SPLIT
    part = wx // SPLIT
    cross = min(passes, 2)
    rep = lax.axis_index("rep")
    slab = lax.axis_index("slab")
    z = rep // 2
    y = rep % 2
    partner = rep + 1 - 2 * y
    above = lax.rem(slab + 1, slabs)
    below = lax.rem(slab + slabs - 1, slabs)

    loads = [
        pltpu.make_async_copy(field_ref, own.at[:, 3:3 + depth], load_sem.at[0]),
        pltpu.make_async_copy(mom_ref, mom.at[:, 2:2 + depth], load_sem.at[1]),
    ]
    for copy in loads:
        copy.start()

    barrier = pltpu.get_barrier_semaphore()

    def greet(device):
        pl.semaphore_signal(barrier, inc=1, device_id=device, device_id_type=pl.DeviceIdType.MESH)

    for far in range(1, slabs):
        greet((rep, lax.rem(slab + far, slabs)))
    greet((partner, slab))

    @pl.when(z > 0)
    def _():
        greet((rep - 2, slab))

    @pl.when(z < ROWS - 1)
    def _():
        greet((rep + 2, slab))

    pl.semaphore_wait(barrier, slabs + as_int(z > 0) + as_int(z < ROWS - 1))

    def remote(src, dst, send, recv, device):
        return pltpu.make_async_remote_copy(
            src_ref=src, dst_ref=dst, send_sem=send, recv_sem=recv,
            device_id=device, device_id_type=pl.DeviceIdType.MESH)

    halos = [
        remote(field_ref.at[:, depth - 3:depth], own.at[:, 0:3], halo_s.at[0], halo_r.at[0], (rep, above)),
        remote(field_ref.at[:, 0:3], own.at[:, depth + 3:depth + 6], halo_s.at[1], halo_r.at[1], (rep, below)),
        remote(mom_ref.at[:, depth - 2:depth], mom.at[:, 0:2], halo_s.at[2], halo_r.at[2], (rep, above)),
        remote(mom_ref.at[:, 0:2], mom.at[:, depth + 2:depth + 4], halo_s.at[3], halo_r.at[3], (rep, below)),
    ]
    for copy in halos:
        copy.start()
    moved_halos = [
        remote(moved.at[depth:depth + 3], moved.at[0:3], halo_s.at[4], halo_r.at[4], (rep, above)),
        remote(moved.at[3:6], moved.at[depth + 3:depth + 6], halo_s.at[5], halo_r.at[5], (rep, below)),
    ]

    by_group, slots = wishes(parent_ref)
    mine, other = [], []
    for row in range(ROWS):
        mine.append(jnp.where(y == 0, by_group[2 * row], by_group[2 * row + 1]))
        other.append(jnp.where(y == 0, by_group[2 * row + 1], by_group[2 * row]))
    here, slot = jnp.int32(-1), jnp.int32(0)
    for group in range(2 * ROWS):
        here = jnp.where(rep == group, by_group[group], here)
        slot = jnp.where(rep == group, slots[group], slot)
    here = jnp.where(here >= 0, here, 2 * rep)
    y_out_items = cross_items(other, 2 * rep, cross)
    y_in_items = cross_items(mine, 2 * partner, cross)
    up_out_items = line_items(mine, z, passes, True)
    up_in_items = line_items(mine, z - 1, passes, True)
    dn_out_items = line_items(mine, z, passes, False)
    dn_in_items = line_items(mine, z + 1, passes, False)

    def copy_y(c):
        return remote(y_out.at[c], y_in.at[c], y_s.at[c], y_r.at[c], (partner, slab))

    def copy_up(c):
        return remote(up_out.at[c], up_in.at[c], up_s.at[c], up_r.at[c], (rep + 2, slab))

    def copy_dn(c):
        return remote(dn_out.at[c], dn_in.at[c], dn_s.at[c], dn_r.at[c], (rep - 2, slab))

    def layer_of(c):
        k = c // SPLIT
        return jnp.where(k < 3, k, jnp.where(k < 6, k + depth - 6, k - 3))

    def rows_of(c):
        return pl.ds(pl.multiple_of((c % SPLIT) * part, part), part)

    def own_blocks(c):
        layer, rows = layer_of(c), rows_of(c)
        return [(2 * rep, own[0, 3 + layer, rows]), (2 * rep + 1, own[1, 3 + layer, rows])]

    def cross_blocks(c):
        return [(y_in_items[q], y_in[c, q]) for q in range(cross)]

    def up_blocks(c):
        return [(up_in_items[q], up_in[c, q]) for q in range(passes)]

    def dn_blocks(c):
        return [(dn_in_items[q], dn_in[c, q]) for q in range(passes)]

    def layer_step(k, field_at, mom_at, which, emit):
        k1, k2, k3 = k - 1, jnp.maximum(k - 2, 0), jnp.maximum(k - 3, 0)
        lower, center, upper = field_at(k - 1), field_at(k), field_at(k + 1)
        before, push = mom_at(k - 1), kick[k1]
        mid_low, mid_at = mid[k2], mid[k1]
        end_low, end_at, push_b = end[k3], end[k2], kick_b[k2]
        value, top, right = force(lower, center, upper)
        first = before + (0.5 * step_size) * value
        mid_up = center + step_size * first
        dz, dx, dy = upper - center, top - center, right - center
        square = center * center
        local = 0.5 * (dz * dz + dx * dx + dy * dy)
        local = local + square * (0.5 * mass_square + (0.25 * coupling) * square)
        share = jnp.sum(local.reshape(wx // 8, 8, wy), axis=0)
        value, _, _ = force(mid_low, mid_at, mid_up)
        second = push + step_size * value
        end_up = mid_at + step_size * second
        value, _, _ = force(end_low, end_at, end_up)
        third = push_b + (0.5 * step_size) * value
        sums[which] += jnp.where((k >= 3) & (k < depth + 3), share, 0.0)
        kick[k] = first
        mid[k] = mid_up
        kick_b[k1] = second
        end[k1] = end_up
        emit(jnp.maximum(k - 5, 0), end_at, third)

    sums[...] = jnp.zeros_like(sums)
    loads[0].wait()
    loads[1].wait()
    rest = 1 - slot
    steps = depth + 4
    total = chunks + ROWS * delay
    begin_rest = total - steps
    up_skew = delay * (z + 1)
    dn_skew = delay * (ROWS - z)
    end_skew = jnp.maximum(up_skew, dn_skew)

    def rest_emit(layer, field, momentum):
        rest_f[layer] = field
        rest_m[layer] = momentum

    def during(t, skew):
        return (t >= skew) & (t < skew + chunks)

    def step(t, _):
        @pl.when(t < chunks)
        def _():
            blocks = own_blocks(t)
            for p in range(cross):
                y_out[t, p] = pick(y_out_items[p], blocks)
            copy_y(t).start()

        @pl.when(during(t, delay))
        def _():
            copy_y(t - delay).wait_recv()

        @pl.when(during(t, up_skew) & (z > 0))
        def _():
            copy_up(t - up_skew).wait_recv()

        @pl.when(during(t, dn_skew) & (z < ROWS - 1))
        def _():
            copy_dn(t - dn_skew).wait_recv()

        @pl.when(during(t, up_skew) & (z < ROWS - 1))
        def _():
            c = t - up_skew
            blocks = own_blocks(c) + cross_blocks(c) + up_blocks(c)
            for p in range(passes):
                up_out[c, p] = pick(up_out_items[p], blocks)
            copy_up(c).start()

        @pl.when(during(t, dn_skew) & (z > 0))
        def _():
            c = t - dn_skew
            blocks = own_blocks(c) + cross_blocks(c) + dn_blocks(c)
            for p in range(passes):
                dn_out[c, p] = pick(dn_out_items[p], blocks)
            copy_dn(c).start()

        @pl.when(during(t, end_skew))
        def _():
            c = t - end_skew
            blocks = own_blocks(c) + cross_blocks(c) + up_blocks(c) + dn_blocks(c)
            moved[3 + layer_of(c), rows_of(c)] = pick(here, blocks)

        @pl.when(t == end_skew + 6 * SPLIT - 1)
        def _():
            for copy in moved_halos:
                copy.start()

        @pl.when(t == begin_rest)
        def _():
            for copy in halos:
                copy.wait_recv()

        @pl.when(t >= begin_rest)
        def _():
            layer_step(t - begin_rest + 1, lambda k: own[rest, k], lambda k: mom[rest, k], 0, rest_emit)

        return 0

    lax.fori_loop(0, total, step, 0)
    for copy in moved_halos:
        copy.wait_recv()

    def moved_emit(layer, field, momentum):
        other_f, other_m = rest_f[layer], rest_m[layer]
        out_f[0, layer] = jnp.where(slot == 0, field, other_f)
        out_f[1, layer] = jnp.where(slot == 0, other_f, field)
        out_m[0, layer] = jnp.where(slot == 0, momentum, other_m)
        out_m[1, layer] = jnp.where(slot == 0, other_m, momentum)

    def moved_step(k, _):
        layer_step(k, lambda i: moved[i], lambda i: mom[slot, i], 1, moved_emit)
        return 0

    lax.fori_loop(1, steps + 1, moved_step, 0)

    tiles[0] = jnp.where(slot == 0, sums[1], sums[0])
    tiles[1] = jnp.where(slot == 0, sums[0], sums[1])
    shares = [
        remote(tiles, tiles_in.at[far - 1], act_s.at[far - 1], act_r.at[far - 1],
               (rep, lax.rem(slab + far, slabs)))
        for far in range(1, slabs)
    ]
    for copy in shares:
        copy.start()

    for copy in halos + moved_halos:
        copy.wait_send()

    def drain(c, _):
        copy_y(c).wait_send()

        @pl.when(z < ROWS - 1)
        def _():
            copy_up(c).wait_send()

        @pl.when(z > 0)
        def _():
            copy_dn(c).wait_send()

        return 0

    lax.fori_loop(0, chunks, drain, 0)
    for copy in shares:
        copy.wait()
    whole = tiles[...]
    for far in range(1, slabs):
        whole = whole + tiles_in[far - 1]
    out_a[0] = jnp.sum(whole[0]) * (1.0 / volume)
    out_a[1] = jnp.sum(whole[1]) * (1.0 / volume)


def run(passes, slabs, delay, replica_field, momentum, parent):
    pair, depth, wx, wy = replica_field.shape
    chunks = depth * SPLIT
    part = wx // SPLIT
    cross = min(passes, 2)
    f32 = jnp.float32

    def plane(*lead):
        return pltpu.VMEM((*lead, wx, wy), f32)

    def block(count):
        return pltpu.VMEM((chunks, count, part, wy), f32)

    dma = pltpu.SemaphoreType.DMA
    volume = depth * slabs * wx * wy
    return pl.pallas_call(
        functools.partial(kernel, passes, slabs, delay, volume),
        out_shape=(
            jax.ShapeDtypeStruct(replica_field.shape, f32),
            jax.ShapeDtypeStruct(replica_field.shape, f32),
            jax.ShapeDtypeStruct((pair,), f32),
        ),
        in_specs=[
            pl.BlockSpec(memory_space=pltpu.SMEM),
            pl.BlockSpec(memory_space=pl.ANY),
            pl.BlockSpec(memory_space=pl.ANY),
        ],
        out_specs=(
            pl.BlockSpec(memory_space=pltpu.VMEM),
            pl.BlockSpec(memory_space=pltpu.VMEM),
            pl.BlockSpec(memory_space=pltpu.SMEM),
        ),
        scratch_shapes=[
            plane(pair, depth + 6), plane(depth + 6), plane(pair, depth + 4),
            plane(depth + 6), plane(depth + 6), plane(depth + 6), plane(depth + 6),
            plane(depth), plane(depth),
            pltpu.VMEM((2, 8, wy), f32), pltpu.VMEM((2, 8, wy), f32), pltpu.VMEM((slabs - 1, 2, 8, wy), f32),
            block(cross), block(cross), block(passes), block(passes), block(passes), block(passes),
            dma((2,)), dma((6,)), dma((6,)),
            dma((chunks,)), dma((chunks,)), dma((chunks,)), dma((chunks,)), dma((chunks,)), dma((chunks,)),
            dma((slabs - 1,)), dma((slabs - 1,)),
        ],
        compiler_params=pltpu.CompilerParams(
            collective_id=passes, has_side_effects=True, vmem_limit_bytes=56 * 2**20),
    )(parent, replica_field, momentum)


def routed(replica_field, momentum, parent):
    slabs = lax.axis_size("slab")
    branches = [functools.partial(run, passes, slabs, delay) for passes, delay in ((1, 5), (2, 3), (3, 2))]
    return lax.switch(links_needed(parent) - 1, branches, replica_field, momentum, parent)


def padded(shard, sides, width):
    for axis, dim in sides:
        devices, length = (lax.axis_size(axis), shard.shape[dim])
        up = [(i, (i + 1) % devices) for i in range(devices)]
        down = [(j, i) for i, j in up]
        last = lax.slice_in_dim(shard, length - width, length, axis=dim)
        initial = lax.slice_in_dim(shard, 0, width, axis=dim)
        before = lax.ppermute(last, axis, up)
        after = lax.ppermute(initial, axis, down)
        shard = jnp.concatenate([before, shard, after], axis=dim)
    return shard


def force_inner(extended):
    center = extended[:, 1:-1]
    nearby = extended[:, :-2] + extended[:, 2:]
    nearby = nearby + jnp.roll(center, 1, 2) + jnp.roll(center, -1, 2)
    nearby = nearby + jnp.roll(center, 1, 3) + jnp.roll(center, -1, 3)
    return nearby - 6.0 * center - mass_square * center - coupling * center * center * center


def action_inner(extended):
    center = extended[:, 1:-1]
    along_z = extended[:, 2:] - center
    along_x = jnp.roll(center, -1, 2) - center
    along_y = jnp.roll(center, -1, 3) - center
    local = 0.5 * (along_z * along_z + along_x * along_x + along_y * along_y)
    local = (
        local
        + 0.5 * mass_square * center * center
        + 0.25 * coupling * center * center * center * center
    )
    return jnp.sum(local, axis=(1, 2, 3))


def extend_one(values):
    return padded(values, (("slab", 1),), 1)


def shards(replica_field, momentum, parent):
    per_group = replica_field.shape[0]
    depth = replica_field.shape[1]
    width_x = replica_field.shape[2]
    width_y = replica_field.shape[3]
    flat = replica_field.reshape(per_group, depth, width_x * width_y)
    spread = lax.all_to_all(flat, "rep", split_axis=2, concat_axis=0, tiled=True)
    copied = jnp.take(spread, parent, axis=0)
    returned = lax.all_to_all(copied, "rep", split_axis=0, concat_axis=2, tiled=True)
    field_start = returned.reshape(per_group, depth, width_x, width_y)
    volume = depth * lax.axis_size("slab") * width_x * width_y
    extended = extend_one(field_start)
    partial_action = action_inner(extended)
    half_kick = momentum + 0.5 * step_size * force_inner(extended)
    field_mid = field_start + step_size * half_kick
    kicked = half_kick + step_size * force_inner(extend_one(field_mid))
    field_end = field_mid + step_size * kicked
    momentum_end = kicked + 0.5 * step_size * force_inner(extend_one(field_end))
    density = lax.psum(partial_action, "slab") / volume
    return (field_end, momentum_end, density)


def solution(mesh):
    in_specs = (P("rep", "slab", None, None), P("rep", "slab", None, None), P())
    out_specs = (P("rep", "slab", None, None), P("rep", "slab", None, None), P("rep"))
    plan = routed if mesh.shape["rep"] == 2 * ROWS and mesh.shape["slab"] > 2 else shards
    return jax.shard_map(plan, mesh=mesh, in_specs=in_specs, out_specs=out_specs, check_vma=False)
```

```python
import functools

import jax
import jax.numpy as jnp
from jax import lax
from jax.experimental import pallas as pl
from jax.experimental.pallas import tpu as pltpu
from jax.sharding import PartitionSpec as P

coupling = 0.5
mass_square = -1.0
step_size = 0.15

ROWS = 4
SPLIT = 2


def holder_row(replica):
    return replica // 4


def as_int(flag):
    return jnp.where(flag, 1, 0).astype(jnp.int32)


def line_items(wanted, at, passes, upward):
    items = [jnp.int32(-1)] * passes
    order = range(ROWS - 1, -1, -1) if upward else range(ROWS)
    seen, count = [], jnp.int32(0)
    for dest in order:
        name = wanted[dest]
        row = holder_row(name)
        active = as_int(name >= 0)
        if upward:
            active = active * as_int(dest > at) * as_int(row <= at)
        else:
            active = active * as_int(dest < at) * as_int(row >= at)
        for other in seen:
            active = active * as_int(other != name)
        for p in range(passes):
            items[p] = jnp.where(active * as_int(count == p) == 1, name, items[p])
        count = count + active
        seen.append(name)
    return items


def cross_items(wanted, first, passes):
    need = []
    for local in range(2):
        flag = jnp.int32(0)
        for dest in range(ROWS):
            flag = jnp.maximum(flag, as_int(wanted[dest] == first + local))
        need.append(flag)
    items = [jnp.where(need[0] == 1, first, jnp.where(need[1] == 1, first + 1, -1))]
    if passes > 1:
        items.append(jnp.where(need[0] * need[1] == 1, first + 1, -1))
    return items


def wishes(parent_ref):
    names, slots = [], []
    for group in range(2 * ROWS):
        first, second = parent_ref[2 * group], parent_ref[2 * group + 1]
        names.append(jnp.where(first != 2 * group, first, jnp.where(second != 2 * group + 1, second, -1)))
        slots.append(as_int(second != 2 * group + 1))
    return names, slots


def plan_kernel(parent_ref, out_ref):
    names, _ = wishes(parent_ref)
    most = jnp.int32(1)
    for column in range(2):
        wanted = [names[2 * row + column] for row in range(ROWS)]
        for row in range(ROWS):
            carried = [cross_items(wanted, jnp.int32(4 * row + 2 - 2 * column), 2)]
            carried += [line_items(wanted, row, ROWS - 1, upward) for upward in (True, False)]
            for items in carried:
                for p, item in enumerate(items):
                    most = jnp.where(item >= 0, jnp.maximum(most, p + 1), most)
    out_ref[0] = most


def links_needed(parent):
    smem = pl.BlockSpec(memory_space=pltpu.SMEM)
    return pl.pallas_call(
        plan_kernel, out_shape=jax.ShapeDtypeStruct((1,), jnp.int32), in_specs=[smem], out_specs=smem)(parent)[0]


def pick(name, candidates):
    value = candidates[0][1]
    for other, block in candidates[1:]:
        value = jnp.where(other == name, block, value)
    return value


def force(lower, center, upper):
    top = pltpu.roll(center, center.shape[0] - 1, 0)
    bottom = pltpu.roll(center, 1, 0)
    right = pltpu.roll(center, center.shape[1] - 1, 1)
    left = pltpu.roll(center, 1, 1)
    nearby = (lower + upper) + (top + bottom) + (right + left)
    value = nearby - center * ((6.0 + mass_square) + coupling * (center * center))
    return value, top, right


def action(center, upper, top, right):
    dz, dx, dy = upper - center, top - center, right - center
    square = center * center
    local = 0.5 * (dz * dz + dx * dx + dy * dy)
    local = local + square * (0.5 * mass_square + (0.25 * coupling) * square)
    return jnp.sum(local.reshape(local.shape[0] // 8, 8, local.shape[1]), axis=0)


def kernel(passes, slabs, delay, volume,
           parent_ref, field_ref, mom_ref, out_f, out_m, out_a,
           own, moved, mom, kick, mid, kick_b, end, rest_f, rest_m, res_f, res_m, sums, tiles, tiles_in,
           y_out, y_in, up_out, up_in, dn_out, dn_in,
           load_sem, store_sem, halo_s, halo_r, y_s, y_r, up_s, up_r, dn_s, dn_r, act_s, act_r):
    depth, wx, wy = field_ref.shape[1:]
    chunks = depth * SPLIT
    part = wx // SPLIT
    cross = min(passes, 2)
    rep = lax.axis_index("rep")
    slab = lax.axis_index("slab")
    z = rep // 2
    y = rep % 2
    partner = rep + 1 - 2 * y
    above = lax.rem(slab + 1, slabs)
    below = lax.rem(slab + slabs - 1, slabs)

    loads = [
        pltpu.make_async_copy(field_ref, own.at[:, 3:3 + depth], load_sem.at[0]),
        pltpu.make_async_copy(mom_ref, mom.at[:, 2:2 + depth], load_sem.at[1]),
    ]
    for copy in loads:
        copy.start()

    barrier = pltpu.get_barrier_semaphore()

    def greet(device):
        pl.semaphore_signal(barrier, inc=1, device_id=device, device_id_type=pl.DeviceIdType.MESH)

    for far in range(1, slabs):
        greet((rep, lax.rem(slab + far, slabs)))
    greet((partner, slab))

    @pl.when(z > 0)
    def _():
        greet((rep - 2, slab))

    @pl.when(z < ROWS - 1)
    def _():
        greet((rep + 2, slab))

    pl.semaphore_wait(barrier, slabs + as_int(z > 0) + as_int(z < ROWS - 1))

    def remote(src, dst, send, recv, device):
        return pltpu.make_async_remote_copy(
            src_ref=src, dst_ref=dst, send_sem=send, recv_sem=recv,
            device_id=device, device_id_type=pl.DeviceIdType.MESH)

    halos = [
        remote(field_ref.at[:, depth - 3:depth], own.at[:, 0:3], halo_s.at[0], halo_r.at[0], (rep, above)),
        remote(field_ref.at[:, 0:3], own.at[:, depth + 3:depth + 6], halo_s.at[1], halo_r.at[1], (rep, below)),
        remote(mom_ref.at[:, depth - 2:depth], mom.at[:, 0:2], halo_s.at[2], halo_r.at[2], (rep, above)),
        remote(mom_ref.at[:, 0:2], mom.at[:, depth + 2:depth + 4], halo_s.at[3], halo_r.at[3], (rep, below)),
    ]
    for copy in halos:
        copy.start()
    moved_halos = [
        remote(moved.at[depth:depth + 3], moved.at[0:3], halo_s.at[4], halo_r.at[4], (rep, above)),
        remote(moved.at[3:6], moved.at[depth + 3:depth + 6], halo_s.at[5], halo_r.at[5], (rep, below)),
    ]

    by_group, slots = wishes(parent_ref)
    mine, other = [], []
    for row in range(ROWS):
        mine.append(jnp.where(y == 0, by_group[2 * row], by_group[2 * row + 1]))
        other.append(jnp.where(y == 0, by_group[2 * row + 1], by_group[2 * row]))
    here, slot = jnp.int32(-1), jnp.int32(0)
    for group in range(2 * ROWS):
        here = jnp.where(rep == group, by_group[group], here)
        slot = jnp.where(rep == group, slots[group], slot)
    here = jnp.where(here >= 0, here, 2 * rep)
    y_out_items = cross_items(other, 2 * rep, cross)
    y_in_items = cross_items(mine, 2 * partner, cross)
    up_out_items = line_items(mine, z, passes, True)
    up_in_items = line_items(mine, z - 1, passes, True)
    dn_out_items = line_items(mine, z, passes, False)
    dn_in_items = line_items(mine, z + 1, passes, False)

    def copy_y(c):
        return remote(y_out.at[c], y_in.at[c], y_s.at[c], y_r.at[c], (partner, slab))

    def copy_up(c):
        return remote(up_out.at[c], up_in.at[c], up_s.at[c], up_r.at[c], (rep + 2, slab))

    def copy_dn(c):
        return remote(dn_out.at[c], dn_in.at[c], dn_s.at[c], dn_r.at[c], (rep - 2, slab))

    def layer_of(c):
        k = c // SPLIT
        return jnp.where(k < 3, k, jnp.where(k < 6, k + depth - 6, k - 3))

    def rows_of(c):
        return pl.ds(pl.multiple_of((c % SPLIT) * part, part), part)

    def own_blocks(c):
        layer, rows = layer_of(c), rows_of(c)
        return [(2 * rep, own[0, 3 + layer, rows]), (2 * rep + 1, own[1, 3 + layer, rows])]

    def cross_blocks(c):
        return [(y_in_items[q], y_in[c, q]) for q in range(cross)]

    def up_blocks(c):
        return [(up_in_items[q], up_in[c, q]) for q in range(passes)]

    def dn_blocks(c):
        return [(dn_in_items[q], dn_in[c, q]) for q in range(passes)]

    def layer_step(k, field_at, mom_at, counted, emit):
        k1, k2, k3 = k - 1, jnp.maximum(k - 2, 0), jnp.maximum(k - 3, 0)
        lower, center, upper = field_at(k - 1), field_at(k), field_at(k + 1)
        before, push = mom_at(k - 1), kick[k1]
        mid_low, mid_at = mid[k2], mid[k1]
        end_low, end_at, push_b = end[k3], end[k2], kick_b[k2]
        value, top, right = force(lower, center, upper)
        first = before + (0.5 * step_size) * value
        mid_up = center + step_size * first
        value, _, _ = force(mid_low, mid_at, mid_up)
        second = push + step_size * value
        end_up = mid_at + step_size * second
        value, _, _ = force(end_low, end_at, end_up)
        third = push_b + (0.5 * step_size) * value
        if counted:
            share = action(center, upper, top, right)
            sums[0] += jnp.where((k >= 3) & (k < depth + 3), share, 0.0)
        kick[k] = first
        mid[k] = mid_up
        kick_b[k1] = second
        end[k1] = end_up
        emit(jnp.maximum(k - 5, 0), end_at, third)

    def moved_action(k):
        center, upper = moved[k], moved[k + 1]
        top = pltpu.roll(center, wx - 1, 0)
        right = pltpu.roll(center, wy - 1, 1)
        sums[1] += action(center, upper, top, right)

    sums[...] = jnp.zeros_like(sums)
    loads[0].wait()
    rest = 1 - slot
    steps = depth + 4
    total = chunks + ROWS * delay
    begin_rest = total - steps
    up_skew = delay * (z + 1)
    dn_skew = delay * (ROWS - z)
    end_skew = jnp.maximum(up_skew, dn_skew)

    def rest_emit(layer, field, momentum):
        rest_f[layer] = field
        rest_m[layer] = momentum

    def during(t, skew):
        return (t >= skew) & (t < skew + chunks)

    def step(t, _):
        @pl.when(t < chunks)
        def _():
            blocks = own_blocks(t)
            for p in range(cross):
                y_out[t, p] = pick(y_out_items[p], blocks)
            copy_y(t).start()

        @pl.when(during(t, delay))
        def _():
            copy_y(t - delay).wait_recv()

        @pl.when(during(t, up_skew) & (z > 0))
        def _():
            copy_up(t - up_skew).wait_recv()

        @pl.when(during(t, dn_skew) & (z < ROWS - 1))
        def _():
            copy_dn(t - dn_skew).wait_recv()

        @pl.when(during(t, up_skew) & (z < ROWS - 1))
        def _():
            c = t - up_skew
            blocks = own_blocks(c) + cross_blocks(c) + up_blocks(c)
            for p in range(passes):
                up_out[c, p] = pick(up_out_items[p], blocks)
            copy_up(c).start()

        @pl.when(during(t, dn_skew) & (z > 0))
        def _():
            c = t - dn_skew
            blocks = own_blocks(c) + cross_blocks(c) + dn_blocks(c)
            for p in range(passes):
                dn_out[c, p] = pick(dn_out_items[p], blocks)
            copy_dn(c).start()

        @pl.when(during(t, end_skew))
        def _():
            c = t - end_skew
            blocks = own_blocks(c) + cross_blocks(c) + up_blocks(c) + dn_blocks(c)
            moved[3 + layer_of(c), rows_of(c)] = pick(here, blocks)

            @pl.when((c >= 6 * SPLIT) & (c % SPLIT == SPLIT - 1))
            def _():
                moved_action(c // SPLIT - 1)

        @pl.when(t == end_skew + 6 * SPLIT - 1)
        def _():
            for copy in moved_halos:
                copy.start()

        @pl.when(t == begin_rest)
        def _():
            loads[1].wait()
            for copy in halos:
                copy.wait_recv()

        @pl.when(t >= begin_rest)
        def _():
            layer_step(t - begin_rest + 1, lambda k: own[rest, k], lambda k: mom[rest, k], True, rest_emit)

        return 0

    lax.fori_loop(0, total, step, 0)
    for copy in moved_halos:
        copy.wait_recv()

    def rest_of_action(i, _):
        moved_action(jnp.where(i < 2, i + 3, i + depth - 3))
        return 0

    lax.fori_loop(0, 6, rest_of_action, 0)
    tiles[0] = jnp.where(slot == 0, sums[1], sums[0])
    tiles[1] = jnp.where(slot == 0, sums[0], sums[1])
    shares = [
        remote(tiles, tiles_in.at[far - 1], act_s.at[far - 1], act_r.at[far - 1],
               (rep, lax.rem(slab + far, slabs)))
        for far in range(1, slabs)
    ]
    for copy in shares:
        copy.start()

    def moved_emit(layer, field, momentum):
        other_f, other_m = rest_f[layer], rest_m[layer]
        res_f[0, layer] = jnp.where(slot == 0, field, other_f)
        res_f[1, layer] = jnp.where(slot == 0, other_f, field)
        res_m[0, layer] = jnp.where(slot == 0, momentum, other_m)
        res_m[1, layer] = jnp.where(slot == 0, other_m, momentum)

    group = depth // 4

    def stores(i):
        layers = pl.ds(i * group, group)
        return [
            pltpu.make_async_copy(res_f.at[:, layers], out_f.at[:, layers], store_sem.at[0, i]),
            pltpu.make_async_copy(res_m.at[:, layers], out_m.at[:, layers], store_sem.at[1, i]),
        ]

    def moved_step(k, _):
        layer_step(k, lambda i: moved[i], lambda i: mom[slot, i], False, moved_emit)

        @pl.when((k >= group + 4) & ((k - 4) % group == 0))
        def _():
            for copy in stores((k - 4) // group - 1):
                copy.start()

        return 0

    lax.fori_loop(1, steps + 1, moved_step, 0)

    for copy in halos + moved_halos:
        copy.wait_send()

    def drain(c, _):
        copy_y(c).wait_send()

        @pl.when(z < ROWS - 1)
        def _():
            copy_up(c).wait_send()

        @pl.when(z > 0)
        def _():
            copy_dn(c).wait_send()

        return 0

    lax.fori_loop(0, chunks, drain, 0)
    for i in range(4):
        for copy in stores(i):
            copy.wait()
    for copy in shares:
        copy.wait()
    whole = tiles[...]
    for far in range(1, slabs):
        whole = whole + tiles_in[far - 1]
    out_a[0] = jnp.sum(whole[0]) * (1.0 / volume)
    out_a[1] = jnp.sum(whole[1]) * (1.0 / volume)


def run(passes, slabs, delay, replica_field, momentum, parent):
    pair, depth, wx, wy = replica_field.shape
    chunks = depth * SPLIT
    part = wx // SPLIT
    cross = min(passes, 2)
    f32 = jnp.float32

    def plane(*lead):
        return pltpu.VMEM((*lead, wx, wy), f32)

    def block(count):
        return pltpu.VMEM((chunks, count, part, wy), f32)

    dma = pltpu.SemaphoreType.DMA
    volume = depth * slabs * wx * wy
    return pl.pallas_call(
        functools.partial(kernel, passes, slabs, delay, volume),
        out_shape=(
            jax.ShapeDtypeStruct(replica_field.shape, f32),
            jax.ShapeDtypeStruct(replica_field.shape, f32),
            jax.ShapeDtypeStruct((pair,), f32),
        ),
        in_specs=[
            pl.BlockSpec(memory_space=pltpu.SMEM),
            pl.BlockSpec(memory_space=pl.ANY),
            pl.BlockSpec(memory_space=pl.ANY),
        ],
        out_specs=(
            pl.BlockSpec(memory_space=pl.ANY),
            pl.BlockSpec(memory_space=pl.ANY),
            pl.BlockSpec(memory_space=pltpu.SMEM),
        ),
        scratch_shapes=[
            plane(pair, depth + 6), plane(depth + 6), plane(pair, depth + 4),
            plane(depth + 6), plane(depth + 6), plane(depth + 6), plane(depth + 6),
            plane(depth), plane(depth), plane(pair, depth), plane(pair, depth),
            pltpu.VMEM((2, 8, wy), f32), pltpu.VMEM((2, 8, wy), f32), pltpu.VMEM((slabs - 1, 2, 8, wy), f32),
            block(cross), block(cross), block(passes), block(passes), block(passes), block(passes),
            dma((2,)), dma((2, 4)), dma((6,)), dma((6,)),
            dma((chunks,)), dma((chunks,)), dma((chunks,)), dma((chunks,)), dma((chunks,)), dma((chunks,)),
            dma((slabs - 1,)), dma((slabs - 1,)),
        ],
        compiler_params=pltpu.CompilerParams(
            collective_id=passes, has_side_effects=True, vmem_limit_bytes=56 * 2**20),
    )(parent, replica_field, momentum)


def routed(replica_field, momentum, parent):
    slabs = lax.axis_size("slab")
    branches = [functools.partial(run, passes, slabs, delay) for passes, delay in ((1, 5), (2, 3), (3, 2))]
    return lax.switch(links_needed(parent) - 1, branches, replica_field, momentum, parent)


def padded(shard, sides, width):
    for axis, dim in sides:
        devices, length = (lax.axis_size(axis), shard.shape[dim])
        up = [(i, (i + 1) % devices) for i in range(devices)]
        down = [(j, i) for i, j in up]
        last = lax.slice_in_dim(shard, length - width, length, axis=dim)
        initial = lax.slice_in_dim(shard, 0, width, axis=dim)
        before = lax.ppermute(last, axis, up)
        after = lax.ppermute(initial, axis, down)
        shard = jnp.concatenate([before, shard, after], axis=dim)
    return shard


def force_inner(extended):
    center = extended[:, 1:-1]
    nearby = extended[:, :-2] + extended[:, 2:]
    nearby = nearby + jnp.roll(center, 1, 2) + jnp.roll(center, -1, 2)
    nearby = nearby + jnp.roll(center, 1, 3) + jnp.roll(center, -1, 3)
    return nearby - 6.0 * center - mass_square * center - coupling * center * center * center


def action_inner(extended):
    center = extended[:, 1:-1]
    along_z = extended[:, 2:] - center
    along_x = jnp.roll(center, -1, 2) - center
    along_y = jnp.roll(center, -1, 3) - center
    local = 0.5 * (along_z * along_z + along_x * along_x + along_y * along_y)
    local = (
        local
        + 0.5 * mass_square * center * center
        + 0.25 * coupling * center * center * center * center
    )
    return jnp.sum(local, axis=(1, 2, 3))


def extend_one(values):
    return padded(values, (("slab", 1),), 1)


def shards(replica_field, momentum, parent):
    per_group = replica_field.shape[0]
    depth = replica_field.shape[1]
    width_x = replica_field.shape[2]
    width_y = replica_field.shape[3]
    flat = replica_field.reshape(per_group, depth, width_x * width_y)
    spread = lax.all_to_all(flat, "rep", split_axis=2, concat_axis=0, tiled=True)
    copied = jnp.take(spread, parent, axis=0)
    returned = lax.all_to_all(copied, "rep", split_axis=0, concat_axis=2, tiled=True)
    field_start = returned.reshape(per_group, depth, width_x, width_y)
    volume = depth * lax.axis_size("slab") * width_x * width_y
    extended = extend_one(field_start)
    partial_action = action_inner(extended)
    half_kick = momentum + 0.5 * step_size * force_inner(extended)
    field_mid = field_start + step_size * half_kick
    kicked = half_kick + step_size * force_inner(extend_one(field_mid))
    field_end = field_mid + step_size * kicked
    momentum_end = kicked + 0.5 * step_size * force_inner(extend_one(field_end))
    density = lax.psum(partial_action, "slab") / volume
    return (field_end, momentum_end, density)


def solution(mesh):
    in_specs = (P("rep", "slab", None, None), P("rep", "slab", None, None), P())
    out_specs = (P("rep", "slab", None, None), P("rep", "slab", None, None), P("rep"))
    plan = routed if mesh.shape["rep"] == 2 * ROWS and mesh.shape["slab"] > 2 else shards
    return jax.shard_map(plan, mesh=mesh, in_specs=in_specs, out_specs=out_specs, check_vma=False)
```

```python
import functools

import jax
import jax.numpy as jnp
from jax import lax
from jax.experimental import pallas as pl
from jax.experimental.pallas import tpu as pltpu
from jax.sharding import PartitionSpec as P

coupling = 0.5
mass_square = -1.0
step_size = 0.15

ROWS = 4
SPLIT = 2


def holder_row(replica):
    return replica // 4


def holder_column(replica):
    return (replica // 2) % 2


def as_int(flag):
    return jnp.where(flag, 1, 0).astype(jnp.int32)


def line_items(wanted, at, passes, upward):
    items = [jnp.int32(-1)] * passes
    seen, count = [], jnp.int32(0)
    for dest, name in sorted(wanted, key=lambda pair: -pair[0] if upward else pair[0]):
        row = holder_row(name)
        active = as_int(name >= 0)
        if upward:
            active = active * as_int(dest > at) * as_int(row <= at)
        else:
            active = active * as_int(dest < at) * as_int(row >= at)
        for other in seen:
            active = active * as_int(other != name)
        for p in range(passes):
            items[p] = jnp.where(active * as_int(count == p) == 1, name, items[p])
        count = count + active
        seen.append(name)
    return items


def held_in(names, column):
    return [(group // 2, jnp.where(holder_column(name) == column, name, -1)) for group, name in enumerate(names)]


def cross_items(wanted, first, passes):
    need = []
    for local in range(2):
        flag = jnp.int32(0)
        for dest in range(ROWS):
            flag = jnp.maximum(flag, as_int(wanted[dest] == first + local))
        need.append(flag)
    items = [jnp.where(need[0] == 1, first, jnp.where(need[1] == 1, first + 1, -1))]
    if passes > 1:
        items.append(jnp.where(need[0] * need[1] == 1, first + 1, -1))
    return items


def wishes(parent_ref):
    names, slots = [], []
    for group in range(2 * ROWS):
        first, second = parent_ref[2 * group], parent_ref[2 * group + 1]
        names.append(jnp.where(first != 2 * group, first, jnp.where(second != 2 * group + 1, second, -1)))
        slots.append(as_int(second != 2 * group + 1))
    return names, slots


def plan_kernel(parent_ref, out_ref):
    names, _ = wishes(parent_ref)
    y_first, z_first = jnp.int32(1), jnp.int32(1)
    for column in range(2):
        wanted = [names[2 * row + column] for row in range(ROWS)]
        by_row = list(enumerate(wanted))
        held = held_in(names, column)
        for row in range(ROWS):
            carried = [cross_items(wanted, jnp.int32(4 * row + 2 - 2 * column), 2)]
            carried += [line_items(by_row, row, ROWS - 1, upward) for upward in (True, False)]
            for items in carried:
                for p, item in enumerate(items):
                    y_first = jnp.where(item >= 0, jnp.maximum(y_first, p + 1), y_first)
            for upward in (True, False):
                for p, item in enumerate(line_items(held, row, 2, upward)):
                    z_first = jnp.where(item >= 0, jnp.maximum(z_first, p + 1), z_first)
    out_ref[0] = jnp.where(y_first == 1, 0, jnp.where(z_first == 1, 1, y_first))


def plan_for(parent):
    smem = pl.BlockSpec(memory_space=pltpu.SMEM)
    return pl.pallas_call(
        plan_kernel, out_shape=jax.ShapeDtypeStruct((1,), jnp.int32), in_specs=[smem], out_specs=smem)(parent)[0]


def pick(name, candidates):
    value = candidates[0][1]
    for other, block in candidates[1:]:
        value = jnp.where(other == name, block, value)
    return value


def force(lower, center, upper):
    top = pltpu.roll(center, center.shape[0] - 1, 0)
    bottom = pltpu.roll(center, 1, 0)
    right = pltpu.roll(center, center.shape[1] - 1, 1)
    left = pltpu.roll(center, 1, 1)
    nearby = (lower + upper) + (top + bottom) + (right + left)
    value = nearby - center * ((6.0 + mass_square) + coupling * (center * center))
    return value, top, right


def action(center, upper, top, right):
    dz, dx, dy = upper - center, top - center, right - center
    square = center * center
    local = 0.5 * (dz * dz + dx * dx + dy * dy)
    local = local + square * (0.5 * mass_square + (0.25 * coupling) * square)
    return jnp.sum(local.reshape(local.shape[0] // 8, 8, local.shape[1]), axis=0)


def kernel(passes, y_first, slabs, delay, volume,
           parent_ref, field_ref, mom_ref, out_f, out_m, out_a,
           own, moved, mom, kick, mid, kick_b, end, rest_f, rest_m, res_f, res_m, sums, tiles, tiles_in,
           y_out, y_in, up_out, up_in, dn_out, dn_in,
           load_sem, store_sem, halo_s, halo_r, y_s, y_r, up_s, up_r, dn_s, dn_r, act_s, act_r):
    depth, wx, wy = field_ref.shape[1:]
    chunks = depth * SPLIT
    part = wx // SPLIT
    cross = min(passes, 2) if y_first else 1
    rep = lax.axis_index("rep")
    slab = lax.axis_index("slab")
    z = rep // 2
    y = rep % 2
    partner = rep + 1 - 2 * y
    above = lax.rem(slab + 1, slabs)
    below = lax.rem(slab + slabs - 1, slabs)

    loads = [
        pltpu.make_async_copy(field_ref, own.at[:, 3:3 + depth], load_sem.at[0]),
        pltpu.make_async_copy(mom_ref, mom.at[:, 2:2 + depth], load_sem.at[1]),
    ]
    for copy in loads:
        copy.start()

    barrier = pltpu.get_barrier_semaphore()

    def greet(device):
        pl.semaphore_signal(barrier, inc=1, device_id=device, device_id_type=pl.DeviceIdType.MESH)

    for far in range(1, slabs):
        greet((rep, lax.rem(slab + far, slabs)))
    greet((partner, slab))

    @pl.when(z > 0)
    def _():
        greet((rep - 2, slab))

    @pl.when(z < ROWS - 1)
    def _():
        greet((rep + 2, slab))

    pl.semaphore_wait(barrier, slabs + as_int(z > 0) + as_int(z < ROWS - 1))

    def remote(src, dst, send, recv, device):
        return pltpu.make_async_remote_copy(
            src_ref=src, dst_ref=dst, send_sem=send, recv_sem=recv,
            device_id=device, device_id_type=pl.DeviceIdType.MESH)

    halos = [
        remote(field_ref.at[:, depth - 3:depth], own.at[:, 0:3], halo_s.at[0], halo_r.at[0], (rep, above)),
        remote(field_ref.at[:, 0:3], own.at[:, depth + 3:depth + 6], halo_s.at[1], halo_r.at[1], (rep, below)),
        remote(mom_ref.at[:, depth - 2:depth], mom.at[:, 0:2], halo_s.at[2], halo_r.at[2], (rep, above)),
        remote(mom_ref.at[:, 0:2], mom.at[:, depth + 2:depth + 4], halo_s.at[3], halo_r.at[3], (rep, below)),
    ]
    for copy in halos:
        copy.start()
    moved_halos = [
        remote(moved.at[depth:depth + 3], moved.at[0:3], halo_s.at[4], halo_r.at[4], (rep, above)),
        remote(moved.at[3:6], moved.at[depth + 3:depth + 6], halo_s.at[5], halo_r.at[5], (rep, below)),
    ]

    by_group, slots = wishes(parent_ref)
    here, there, slot = jnp.int32(-1), jnp.int32(-1), jnp.int32(0)
    for group in range(2 * ROWS):
        here = jnp.where(rep == group, by_group[group], here)
        there = jnp.where(partner == group, by_group[group], there)
        slot = jnp.where(rep == group, slots[group], slot)
    if y_first:
        mine = [jnp.where(y == 0, by_group[2 * row], by_group[2 * row + 1]) for row in range(ROWS)]
        other = [jnp.where(y == 0, by_group[2 * row + 1], by_group[2 * row]) for row in range(ROWS)]
        y_out_items = cross_items(other, 2 * rep, cross)
        y_in_items = cross_items(mine, 2 * partner, cross)
        wanted = list(enumerate(mine))
    else:
        y_out_items = [jnp.where(holder_column(there) == y, there, -1)]
        y_in_items = [jnp.where(holder_column(here) == y, -1, here)]
        wanted = held_in(by_group, y)
    here = jnp.where(here >= 0, here, 2 * rep)
    up_out_items = line_items(wanted, z, passes, True)
    up_in_items = line_items(wanted, z - 1, passes, True)
    dn_out_items = line_items(wanted, z, passes, False)
    dn_in_items = line_items(wanted, z + 1, passes, False)

    def copy_y(c):
        return remote(y_out.at[c], y_in.at[c], y_s.at[c], y_r.at[c], (partner, slab))

    def copy_up(c):
        return remote(up_out.at[c], up_in.at[c], up_s.at[c], up_r.at[c], (rep + 2, slab))

    def copy_dn(c):
        return remote(dn_out.at[c], dn_in.at[c], dn_s.at[c], dn_r.at[c], (rep - 2, slab))

    def layer_of(c):
        k = c // SPLIT
        return jnp.where(k < 3, k, jnp.where(k < 6, k + depth - 6, k - 3))

    def rows_of(c):
        return pl.ds(pl.multiple_of((c % SPLIT) * part, part), part)

    def own_blocks(c):
        layer, rows = layer_of(c), rows_of(c)
        return [(2 * rep, own[0, 3 + layer, rows]), (2 * rep + 1, own[1, 3 + layer, rows])]

    def cross_blocks(c):
        return [(y_in_items[q], y_in[c, q]) for q in range(cross)]

    def up_blocks(c):
        return [(up_in_items[q], up_in[c, q]) for q in range(passes)]

    def dn_blocks(c):
        return [(dn_in_items[q], dn_in[c, q]) for q in range(passes)]

    def layer_step(k, field_at, mom_at, counted, emit):
        k1, k2, k3 = k - 1, jnp.maximum(k - 2, 0), jnp.maximum(k - 3, 0)
        lower, center, upper = field_at(k - 1), field_at(k), field_at(k + 1)
        before, push = mom_at(k - 1), kick[k1]
        mid_low, mid_at = mid[k2], mid[k1]
        end_low, end_at, push_b = end[k3], end[k2], kick_b[k2]
        value, top, right = force(lower, center, upper)
        first = before + (0.5 * step_size) * value
        mid_up = center + step_size * first
        value, _, _ = force(mid_low, mid_at, mid_up)
        second = push + step_size * value
        end_up = mid_at + step_size * second
        value, _, _ = force(end_low, end_at, end_up)
        third = push_b + (0.5 * step_size) * value
        if counted:
            share = action(center, upper, top, right)
            sums[0] += jnp.where((k >= 3) & (k < depth + 3), share, 0.0)
        kick[k] = first
        mid[k] = mid_up
        kick_b[k1] = second
        end[k1] = end_up
        emit(jnp.maximum(k - 5, 0), end_at, third)

    def moved_action(k):
        center, upper = moved[k], moved[k + 1]
        top = pltpu.roll(center, wx - 1, 0)
        right = pltpu.roll(center, wy - 1, 1)
        sums[1] += action(center, upper, top, right)

    sums[...] = jnp.zeros_like(sums)
    loads[0].wait()
    rest = 1 - slot
    steps = depth + 4
    total = chunks + ROWS * delay
    begin_rest = total - steps
    farther = jnp.maximum(z, ROWS - 1 - z)
    end_skew = delay * (farther + 1)
    if y_first:
        y_skew, y_wait, up_skew, dn_skew = 0, delay, delay * (z + 1), delay * (ROWS - z)
    else:
        y_skew, y_wait, up_skew, dn_skew = delay * farther, end_skew, delay * z, delay * (ROWS - 1 - z)

    def rest_emit(layer, field, momentum):
        rest_f[layer] = field
        rest_m[layer] = momentum

    def during(t, skew):
        return (t >= skew) & (t < skew + chunks)

    def step(t, _):
        @pl.when(during(t, y_wait))
        def _():
            copy_y(t - y_wait).wait_recv()

        @pl.when(during(t, up_skew) & (z > 0))
        def _():
            copy_up(t - up_skew).wait_recv()

        @pl.when(during(t, dn_skew) & (z < ROWS - 1))
        def _():
            copy_dn(t - dn_skew).wait_recv()

        @pl.when(during(t, y_skew))
        def _():
            c = t - y_skew
            blocks = own_blocks(c) + ([] if y_first else up_blocks(c) + dn_blocks(c))
            for p in range(cross):
                y_out[c, p] = pick(y_out_items[p], blocks)
            copy_y(c).start()

        @pl.when(during(t, up_skew) & (z < ROWS - 1))
        def _():
            c = t - up_skew
            blocks = own_blocks(c) + (cross_blocks(c) if y_first else []) + up_blocks(c)
            for p in range(passes):
                up_out[c, p] = pick(up_out_items[p], blocks)
            copy_up(c).start()

        @pl.when(during(t, dn_skew) & (z > 0))
        def _():
            c = t - dn_skew
            blocks = own_blocks(c) + (cross_blocks(c) if y_first else []) + dn_blocks(c)
            for p in range(passes):
                dn_out[c, p] = pick(dn_out_items[p], blocks)
            copy_dn(c).start()

        @pl.when(during(t, end_skew))
        def _():
            c = t - end_skew
            blocks = own_blocks(c) + cross_blocks(c) + up_blocks(c) + dn_blocks(c)
            moved[3 + layer_of(c), rows_of(c)] = pick(here, blocks)

            @pl.when((c >= 6 * SPLIT) & (c % SPLIT == SPLIT - 1))
            def _():
                moved_action(c // SPLIT - 1)

        @pl.when(t == end_skew + 6 * SPLIT - 1)
        def _():
            for copy in moved_halos:
                copy.start()

        @pl.when(t == begin_rest)
        def _():
            loads[1].wait()
            for copy in halos:
                copy.wait_recv()

        @pl.when(t >= begin_rest)
        def _():
            layer_step(t - begin_rest + 1, lambda k: own[rest, k], lambda k: mom[rest, k], True, rest_emit)

        return 0

    lax.fori_loop(0, total, step, 0)
    for copy in moved_halos:
        copy.wait_recv()

    def rest_of_action(i, _):
        moved_action(jnp.where(i < 2, i + 3, i + depth - 3))
        return 0

    lax.fori_loop(0, 6, rest_of_action, 0)
    tiles[0] = jnp.where(slot == 0, sums[1], sums[0])
    tiles[1] = jnp.where(slot == 0, sums[0], sums[1])
    shares = [
        remote(tiles, tiles_in.at[far - 1], act_s.at[far - 1], act_r.at[far - 1],
               (rep, lax.rem(slab + far, slabs)))
        for far in range(1, slabs)
    ]
    for copy in shares:
        copy.start()

    def moved_emit(layer, field, momentum):
        other_f, other_m = rest_f[layer], rest_m[layer]
        res_f[0, layer] = jnp.where(slot == 0, field, other_f)
        res_f[1, layer] = jnp.where(slot == 0, other_f, field)
        res_m[0, layer] = jnp.where(slot == 0, momentum, other_m)
        res_m[1, layer] = jnp.where(slot == 0, other_m, momentum)

    group = depth // 4

    def stores(i):
        layers = pl.ds(i * group, group)
        return [
            pltpu.make_async_copy(res_f.at[:, layers], out_f.at[:, layers], store_sem.at[0, i]),
            pltpu.make_async_copy(res_m.at[:, layers], out_m.at[:, layers], store_sem.at[1, i]),
        ]

    def moved_step(k, _):
        layer_step(k, lambda i: moved[i], lambda i: mom[slot, i], False, moved_emit)

        @pl.when((k >= group + 4) & ((k - 4) % group == 0))
        def _():
            for copy in stores((k - 4) // group - 1):
                copy.start()

        return 0

    lax.fori_loop(1, steps + 1, moved_step, 0)

    for copy in halos + moved_halos:
        copy.wait_send()

    def drain(c, _):
        copy_y(c).wait_send()

        @pl.when(z < ROWS - 1)
        def _():
            copy_up(c).wait_send()

        @pl.when(z > 0)
        def _():
            copy_dn(c).wait_send()

        return 0

    lax.fori_loop(0, chunks, drain, 0)
    for i in range(4):
        for copy in stores(i):
            copy.wait()
    for copy in shares:
        copy.wait()
    whole = tiles[...]
    for far in range(1, slabs):
        whole = whole + tiles_in[far - 1]
    out_a[0] = jnp.sum(whole[0]) * (1.0 / volume)
    out_a[1] = jnp.sum(whole[1]) * (1.0 / volume)


def run(passes, y_first, slabs, delay, replica_field, momentum, parent):
    pair, depth, wx, wy = replica_field.shape
    chunks = depth * SPLIT
    part = wx // SPLIT
    cross = min(passes, 2) if y_first else 1
    f32 = jnp.float32

    def plane(*lead):
        return pltpu.VMEM((*lead, wx, wy), f32)

    def block(count):
        return pltpu.VMEM((chunks, count, part, wy), f32)

    dma = pltpu.SemaphoreType.DMA
    volume = depth * slabs * wx * wy
    return pl.pallas_call(
        functools.partial(kernel, passes, y_first, slabs, delay, volume),
        out_shape=(
            jax.ShapeDtypeStruct(replica_field.shape, f32),
            jax.ShapeDtypeStruct(replica_field.shape, f32),
            jax.ShapeDtypeStruct((pair,), f32),
        ),
        in_specs=[
            pl.BlockSpec(memory_space=pltpu.SMEM),
            pl.BlockSpec(memory_space=pl.ANY),
            pl.BlockSpec(memory_space=pl.ANY),
        ],
        out_specs=(
            pl.BlockSpec(memory_space=pl.ANY),
            pl.BlockSpec(memory_space=pl.ANY),
            pl.BlockSpec(memory_space=pltpu.SMEM),
        ),
        scratch_shapes=[
            plane(pair, depth + 6), plane(depth + 6), plane(pair, depth + 4),
            plane(depth + 6), plane(depth + 6), plane(depth + 6), plane(depth + 6),
            plane(depth), plane(depth), plane(pair, depth), plane(pair, depth),
            pltpu.VMEM((2, 8, wy), f32), pltpu.VMEM((2, 8, wy), f32), pltpu.VMEM((slabs - 1, 2, 8, wy), f32),
            block(cross), block(cross), block(passes), block(passes), block(passes), block(passes),
            dma((2,)), dma((2, 4)), dma((6,)), dma((6,)),
            dma((chunks,)), dma((chunks,)), dma((chunks,)), dma((chunks,)), dma((chunks,)), dma((chunks,)),
            dma((slabs - 1,)), dma((slabs - 1,)),
        ],
        compiler_params=pltpu.CompilerParams(
            collective_id=passes + (0 if y_first else ROWS), has_side_effects=True, vmem_limit_bytes=56 * 2**20),
    )(parent, replica_field, momentum)


def routed(replica_field, momentum, parent):
    slabs = lax.axis_size("slab")
    plans = ((1, True, 5), (1, False, 5), (2, True, 3), (3, True, 2))
    branches = [functools.partial(run, passes, y_first, slabs, delay) for passes, y_first, delay in plans]
    return lax.switch(plan_for(parent), branches, replica_field, momentum, parent)


def padded(shard, sides, width):
    for axis, dim in sides:
        devices, length = (lax.axis_size(axis), shard.shape[dim])
        up = [(i, (i + 1) % devices) for i in range(devices)]
        down = [(j, i) for i, j in up]
        last = lax.slice_in_dim(shard, length - width, length, axis=dim)
        initial = lax.slice_in_dim(shard, 0, width, axis=dim)
        before = lax.ppermute(last, axis, up)
        after = lax.ppermute(initial, axis, down)
        shard = jnp.concatenate([before, shard, after], axis=dim)
    return shard


def force_inner(extended):
    center = extended[:, 1:-1]
    nearby = extended[:, :-2] + extended[:, 2:]
    nearby = nearby + jnp.roll(center, 1, 2) + jnp.roll(center, -1, 2)
    nearby = nearby + jnp.roll(center, 1, 3) + jnp.roll(center, -1, 3)
    return nearby - 6.0 * center - mass_square * center - coupling * center * center * center


def action_inner(extended):
    center = extended[:, 1:-1]
    along_z = extended[:, 2:] - center
    along_x = jnp.roll(center, -1, 2) - center
    along_y = jnp.roll(center, -1, 3) - center
    local = 0.5 * (along_z * along_z + along_x * along_x + along_y * along_y)
    local = (
        local
        + 0.5 * mass_square * center * center
        + 0.25 * coupling * center * center * center * center
    )
    return jnp.sum(local, axis=(1, 2, 3))


def extend_one(values):
    return padded(values, (("slab", 1),), 1)


def shards(replica_field, momentum, parent):
    per_group = replica_field.shape[0]
    depth = replica_field.shape[1]
    width_x = replica_field.shape[2]
    width_y = replica_field.shape[3]
    flat = replica_field.reshape(per_group, depth, width_x * width_y)
    spread = lax.all_to_all(flat, "rep", split_axis=2, concat_axis=0, tiled=True)
    copied = jnp.take(spread, parent, axis=0)
    returned = lax.all_to_all(copied, "rep", split_axis=0, concat_axis=2, tiled=True)
    field_start = returned.reshape(per_group, depth, width_x, width_y)
    volume = depth * lax.axis_size("slab") * width_x * width_y
    extended = extend_one(field_start)
    partial_action = action_inner(extended)
    half_kick = momentum + 0.5 * step_size * force_inner(extended)
    field_mid = field_start + step_size * half_kick
    kicked = half_kick + step_size * force_inner(extend_one(field_mid))
    field_end = field_mid + step_size * kicked
    momentum_end = kicked + 0.5 * step_size * force_inner(extend_one(field_end))
    density = lax.psum(partial_action, "slab") / volume
    return (field_end, momentum_end, density)


def solution(mesh):
    in_specs = (P("rep", "slab", None, None), P("rep", "slab", None, None), P())
    out_specs = (P("rep", "slab", None, None), P("rep", "slab", None, None), P("rep"))
    plan = routed if mesh.shape["rep"] == 2 * ROWS and mesh.shape["slab"] > 2 else shards
    return jax.shard_map(plan, mesh=mesh, in_specs=in_specs, out_specs=out_specs, check_vma=False)
```

```python
import functools

import jax
import jax.numpy as jnp
from jax import lax
from jax.experimental import pallas as pl
from jax.experimental.pallas import tpu as pltpu
from jax.sharding import PartitionSpec as P

coupling = 0.5
mass_square = -1.0
step_size = 0.15

ROWS = 4
SPLIT = 2


def holder_row(replica):
    return replica // 4


def holder_column(replica):
    return (replica // 2) % 2


def as_int(flag):
    return jnp.where(flag, 1, 0).astype(jnp.int32)


def line_items(wanted, at, passes, upward):
    items = [jnp.int32(-1)] * passes
    seen, count = [], jnp.int32(0)
    for dest, name in sorted(wanted, key=lambda pair: -pair[0] if upward else pair[0]):
        row = holder_row(name)
        active = as_int(name >= 0)
        if upward:
            active = active * as_int(dest > at) * as_int(row <= at)
        else:
            active = active * as_int(dest < at) * as_int(row >= at)
        for other in seen:
            active = active * as_int(other != name)
        for p in range(passes):
            items[p] = jnp.where(active * as_int(count == p) == 1, name, items[p])
        count = count + active
        seen.append(name)
    return items


def held_in(names, column):
    return [(group // 2, jnp.where(holder_column(name) == column, name, -1)) for group, name in enumerate(names)]


def cross_items(wanted, first, passes):
    need = []
    for local in range(2):
        flag = jnp.int32(0)
        for dest in range(ROWS):
            flag = jnp.maximum(flag, as_int(wanted[dest] == first + local))
        need.append(flag)
    items = [jnp.where(need[0] == 1, first, jnp.where(need[1] == 1, first + 1, -1))]
    if passes > 1:
        items.append(jnp.where(need[0] * need[1] == 1, first + 1, -1))
    return items


def wishes(parent_ref):
    names, slots = [], []
    for group in range(2 * ROWS):
        first, second = parent_ref[2 * group], parent_ref[2 * group + 1]
        names.append(jnp.where(first != 2 * group, first, jnp.where(second != 2 * group + 1, second, -1)))
        slots.append(as_int(second != 2 * group + 1))
    return names, slots


def plan_kernel(parent_ref, out_ref):
    names, _ = wishes(parent_ref)
    y_first, z_first = jnp.int32(1), jnp.int32(1)
    for column in range(2):
        wanted = [names[2 * row + column] for row in range(ROWS)]
        by_row = list(enumerate(wanted))
        held = held_in(names, column)
        for row in range(ROWS):
            carried = [cross_items(wanted, jnp.int32(4 * row + 2 - 2 * column), 2)]
            carried += [line_items(by_row, row, ROWS - 1, upward) for upward in (True, False)]
            for items in carried:
                for p, item in enumerate(items):
                    y_first = jnp.where(item >= 0, jnp.maximum(y_first, p + 1), y_first)
            for upward in (True, False):
                for p, item in enumerate(line_items(held, row, 2, upward)):
                    z_first = jnp.where(item >= 0, jnp.maximum(z_first, p + 1), z_first)
    out_ref[0] = jnp.where(y_first == 1, 0, jnp.where(z_first == 1, 1, y_first))


def plan_for(parent):
    smem = pl.BlockSpec(memory_space=pltpu.SMEM)
    return pl.pallas_call(
        plan_kernel, out_shape=jax.ShapeDtypeStruct((1,), jnp.int32), in_specs=[smem], out_specs=smem)(parent)[0]


def pick(name, candidates):
    value = candidates[0][1]
    for other, block in candidates[1:]:
        value = jnp.where(other == name, block, value)
    return value


def force(lower, center, upper):
    top = pltpu.roll(center, center.shape[0] - 1, 0)
    bottom = pltpu.roll(center, 1, 0)
    right = pltpu.roll(center, center.shape[1] - 1, 1)
    left = pltpu.roll(center, 1, 1)
    nearby = (lower + upper) + (top + bottom) + (right + left)
    value = nearby - center * ((6.0 + mass_square) + coupling * (center * center))
    return value, top, right


def action(center, upper, top, right):
    dz, dx, dy = upper - center, top - center, right - center
    square = center * center
    local = 0.5 * (dz * dz + dx * dx + dy * dy)
    local = local + square * (0.5 * mass_square + (0.25 * coupling) * square)
    return jnp.sum(local.reshape(local.shape[0] // 8, 8, local.shape[1]), axis=0)


def kernel(passes, y_first, slabs, delay, volume,
           parent_ref, field_ref, mom_ref, out_f, out_m, out_a,
           own, moved, mom, kick, mid, kick_b, end, rest_f, rest_m, res_f, res_m, sums, tiles, tiles_in,
           y_out, y_in, up_out, up_in, dn_out, dn_in,
           load_sem, store_sem, halo_s, halo_r, y_s, y_r, up_s, up_r, dn_s, dn_r, act_s, act_r):
    depth, wx, wy = field_ref.shape[1:]
    chunks = depth * SPLIT
    part = wx // SPLIT
    cross = min(passes, 2) if y_first else 1
    rep = lax.axis_index("rep")
    slab = lax.axis_index("slab")
    z = rep // 2
    y = rep % 2
    partner = rep + 1 - 2 * y
    above = lax.rem(slab + 1, slabs)
    below = lax.rem(slab + slabs - 1, slabs)

    loads = [
        pltpu.make_async_copy(field_ref, own.at[:, 3:3 + depth], load_sem.at[0]),
        pltpu.make_async_copy(mom_ref, mom.at[:, 2:2 + depth], load_sem.at[1]),
    ]
    for copy in loads:
        copy.start()

    barrier = pltpu.get_barrier_semaphore()

    def greet(device):
        pl.semaphore_signal(barrier, inc=1, device_id=device, device_id_type=pl.DeviceIdType.MESH)

    for far in range(1, slabs):
        greet((rep, lax.rem(slab + far, slabs)))
    greet((partner, slab))

    @pl.when(z > 0)
    def _():
        greet((rep - 2, slab))

    @pl.when(z < ROWS - 1)
    def _():
        greet((rep + 2, slab))

    by_group, slots = wishes(parent_ref)
    here, there, slot = jnp.int32(-1), jnp.int32(-1), jnp.int32(0)
    for group in range(2 * ROWS):
        here = jnp.where(rep == group, by_group[group], here)
        there = jnp.where(partner == group, by_group[group], there)
        slot = jnp.where(rep == group, slots[group], slot)
    if y_first:
        mine = [jnp.where(y == 0, by_group[2 * row], by_group[2 * row + 1]) for row in range(ROWS)]
        other = [jnp.where(y == 0, by_group[2 * row + 1], by_group[2 * row]) for row in range(ROWS)]
        y_out_items = cross_items(other, 2 * rep, cross)
        y_in_items = cross_items(mine, 2 * partner, cross)
        wanted = list(enumerate(mine))
    else:
        y_out_items = [jnp.where(holder_column(there) == y, there, -1)]
        y_in_items = [jnp.where(holder_column(here) == y, -1, here)]
        wanted = held_in(by_group, y)
    here = jnp.where(here >= 0, here, 2 * rep)
    up_out_items = line_items(wanted, z, passes, True)
    up_in_items = line_items(wanted, z - 1, passes, True)
    dn_out_items = line_items(wanted, z, passes, False)
    dn_in_items = line_items(wanted, z + 1, passes, False)

    pl.semaphore_wait(barrier, slabs + as_int(z > 0) + as_int(z < ROWS - 1))

    def remote(src, dst, send, recv, device):
        return pltpu.make_async_remote_copy(
            src_ref=src, dst_ref=dst, send_sem=send, recv_sem=recv,
            device_id=device, device_id_type=pl.DeviceIdType.MESH)

    halos = [
        remote(field_ref.at[:, depth - 3:depth], own.at[:, 0:3], halo_s.at[0], halo_r.at[0], (rep, above)),
        remote(field_ref.at[:, 0:3], own.at[:, depth + 3:depth + 6], halo_s.at[1], halo_r.at[1], (rep, below)),
        remote(mom_ref.at[:, depth - 2:depth], mom.at[:, 0:2], halo_s.at[2], halo_r.at[2], (rep, above)),
        remote(mom_ref.at[:, 0:2], mom.at[:, depth + 2:depth + 4], halo_s.at[3], halo_r.at[3], (rep, below)),
    ]
    for copy in halos:
        copy.start()
    moved_halos = [
        remote(moved.at[depth:depth + 3], moved.at[0:3], halo_s.at[4], halo_r.at[4], (rep, above)),
        remote(moved.at[3:6], moved.at[depth + 3:depth + 6], halo_s.at[5], halo_r.at[5], (rep, below)),
    ]

    def copy_y(c):
        return remote(y_out.at[c], y_in.at[c], y_s.at[c], y_r.at[c], (partner, slab))

    def copy_up(c):
        return remote(up_out.at[c], up_in.at[c], up_s.at[c], up_r.at[c], (rep + 2, slab))

    def copy_dn(c):
        return remote(dn_out.at[c], dn_in.at[c], dn_s.at[c], dn_r.at[c], (rep - 2, slab))

    def layer_of(c):
        k = c // SPLIT
        return jnp.where(k < 3, k, jnp.where(k < 6, k + depth - 6, k - 3))

    def rows_of(c):
        return pl.ds(pl.multiple_of((c % SPLIT) * part, part), part)

    def own_blocks(c):
        layer, rows = layer_of(c), rows_of(c)
        return [(2 * rep, own[0, 3 + layer, rows]), (2 * rep + 1, own[1, 3 + layer, rows])]

    def cross_blocks(c):
        return [(y_in_items[q], y_in[c, q]) for q in range(cross)]

    def up_blocks(c):
        return [(up_in_items[q], up_in[c, q]) for q in range(passes)]

    def dn_blocks(c):
        return [(dn_in_items[q], dn_in[c, q]) for q in range(passes)]

    def layer_step(k, field_at, mom_at, counted, emit):
        k1, k2, k3 = k - 1, jnp.maximum(k - 2, 0), jnp.maximum(k - 3, 0)
        lower, center, upper = field_at(k - 1), field_at(k), field_at(k + 1)
        before, push = mom_at(k - 1), kick[k1]
        mid_low, mid_at = mid[k2], mid[k1]
        end_low, end_at, push_b = end[k3], end[k2], kick_b[k2]
        value, top, right = force(lower, center, upper)
        first = before + (0.5 * step_size) * value
        mid_up = center + step_size * first
        value, _, _ = force(mid_low, mid_at, mid_up)
        second = push + step_size * value
        end_up = mid_at + step_size * second
        value, _, _ = force(end_low, end_at, end_up)
        third = push_b + (0.5 * step_size) * value
        if counted:
            share = action(center, upper, top, right)
            sums[0] += jnp.where((k >= 3) & (k < depth + 3), share, 0.0)
        kick[k] = first
        mid[k] = mid_up
        kick_b[k1] = second
        end[k1] = end_up
        emit(jnp.maximum(k - 5, 0), end_at, third)

    def moved_action(k):
        center, upper = moved[k], moved[k + 1]
        top = pltpu.roll(center, wx - 1, 0)
        right = pltpu.roll(center, wy - 1, 1)
        sums[1] += action(center, upper, top, right)

    sums[...] = jnp.zeros_like(sums)
    loads[0].wait()
    rest = 1 - slot
    steps = depth + 4
    total = chunks + ROWS * delay
    begin_rest = total - steps
    farther = jnp.maximum(z, ROWS - 1 - z)
    end_skew = delay * (farther + 1)
    if y_first:
        y_skew, y_wait, up_skew, dn_skew = 0, delay, delay * (z + 1), delay * (ROWS - z)
    else:
        y_skew, y_wait, up_skew, dn_skew = delay * farther, end_skew, delay * z, delay * (ROWS - 1 - z)

    def rest_emit(layer, field, momentum):
        rest_f[layer] = field
        rest_m[layer] = momentum

    def during(t, skew):
        return (t >= skew) & (t < skew + chunks)

    def step(t, _):
        @pl.when(during(t, y_wait))
        def _():
            copy_y(t - y_wait).wait_recv()

        @pl.when(during(t, up_skew) & (z > 0))
        def _():
            copy_up(t - up_skew).wait_recv()

        @pl.when(during(t, dn_skew) & (z < ROWS - 1))
        def _():
            copy_dn(t - dn_skew).wait_recv()

        @pl.when(during(t, y_skew))
        def _():
            c = t - y_skew
            blocks = own_blocks(c) + ([] if y_first else up_blocks(c) + dn_blocks(c))
            for p in range(cross):
                y_out[c, p] = pick(y_out_items[p], blocks)
            copy_y(c).start()

        @pl.when(during(t, up_skew) & (z < ROWS - 1))
        def _():
            c = t - up_skew
            blocks = own_blocks(c) + (cross_blocks(c) if y_first else []) + up_blocks(c)
            for p in range(passes):
                up_out[c, p] = pick(up_out_items[p], blocks)
            copy_up(c).start()

        @pl.when(during(t, dn_skew) & (z > 0))
        def _():
            c = t - dn_skew
            blocks = own_blocks(c) + (cross_blocks(c) if y_first else []) + dn_blocks(c)
            for p in range(passes):
                dn_out[c, p] = pick(dn_out_items[p], blocks)
            copy_dn(c).start()

        @pl.when(during(t, end_skew))
        def _():
            c = t - end_skew
            blocks = own_blocks(c) + cross_blocks(c) + up_blocks(c) + dn_blocks(c)
            moved[3 + layer_of(c), rows_of(c)] = pick(here, blocks)

            @pl.when((c >= 6 * SPLIT) & (c % SPLIT == SPLIT - 1))
            def _():
                moved_action(c // SPLIT - 1)

        @pl.when(t == end_skew + 6 * SPLIT - 1)
        def _():
            for copy in moved_halos:
                copy.start()

        @pl.when(t == begin_rest)
        def _():
            loads[1].wait()
            for copy in halos:
                copy.wait_recv()

        @pl.when(t >= begin_rest)
        def _():
            layer_step(t - begin_rest + 1, lambda k: own[rest, k], lambda k: mom[rest, k], True, rest_emit)

        return 0

    lax.fori_loop(0, total, step, 0)
    for copy in moved_halos:
        copy.wait_recv()

    def rest_of_action(i, _):
        moved_action(jnp.where(i < 2, i + 3, i + depth - 3))
        return 0

    lax.fori_loop(0, 6, rest_of_action, 0)
    tiles[0] = jnp.where(slot == 0, sums[1], sums[0])
    tiles[1] = jnp.where(slot == 0, sums[0], sums[1])
    shares = [
        remote(tiles, tiles_in.at[far - 1], act_s.at[far - 1], act_r.at[far - 1],
               (rep, lax.rem(slab + far, slabs)))
        for far in range(1, slabs)
    ]
    for copy in shares:
        copy.start()

    def moved_emit(layer, field, momentum):
        other_f, other_m = rest_f[layer], rest_m[layer]
        res_f[0, layer] = jnp.where(slot == 0, field, other_f)
        res_f[1, layer] = jnp.where(slot == 0, other_f, field)
        res_m[0, layer] = jnp.where(slot == 0, momentum, other_m)
        res_m[1, layer] = jnp.where(slot == 0, other_m, momentum)

    group = depth // 4

    def stores(i):
        layers = pl.ds(i * group, group)
        return [
            pltpu.make_async_copy(res_f.at[:, layers], out_f.at[:, layers], store_sem.at[0, i]),
            pltpu.make_async_copy(res_m.at[:, layers], out_m.at[:, layers], store_sem.at[1, i]),
        ]

    def moved_step(k, _):
        layer_step(k, lambda i: moved[i], lambda i: mom[slot, i], False, moved_emit)

        @pl.when((k >= group + 4) & ((k - 4) % group == 0))
        def _():
            for copy in stores((k - 4) // group - 1):
                copy.start()

        return 0

    lax.fori_loop(1, steps + 1, moved_step, 0)

    for copy in halos + moved_halos:
        copy.wait_send()

    def drain(c, _):
        copy_y(c).wait_send()

        @pl.when(z < ROWS - 1)
        def _():
            copy_up(c).wait_send()

        @pl.when(z > 0)
        def _():
            copy_dn(c).wait_send()

        return 0

    lax.fori_loop(0, chunks, drain, 0)
    for i in range(4):
        for copy in stores(i):
            copy.wait()
    for copy in shares:
        copy.wait()
    whole = tiles[...]
    for far in range(1, slabs):
        whole = whole + tiles_in[far - 1]
    out_a[0] = jnp.sum(whole[0]) * (1.0 / volume)
    out_a[1] = jnp.sum(whole[1]) * (1.0 / volume)


def run(passes, y_first, slabs, delay, replica_field, momentum, parent):
    pair, depth, wx, wy = replica_field.shape
    chunks = depth * SPLIT
    part = wx // SPLIT
    cross = min(passes, 2) if y_first else 1
    f32 = jnp.float32

    def plane(*lead):
        return pltpu.VMEM((*lead, wx, wy), f32)

    def block(count):
        return pltpu.VMEM((chunks, count, part, wy), f32)

    dma = pltpu.SemaphoreType.DMA
    volume = depth * slabs * wx * wy
    return pl.pallas_call(
        functools.partial(kernel, passes, y_first, slabs, delay, volume),
        out_shape=(
            jax.ShapeDtypeStruct(replica_field.shape, f32),
            jax.ShapeDtypeStruct(replica_field.shape, f32),
            jax.ShapeDtypeStruct((pair,), f32),
        ),
        in_specs=[
            pl.BlockSpec(memory_space=pltpu.SMEM),
            pl.BlockSpec(memory_space=pl.ANY),
            pl.BlockSpec(memory_space=pl.ANY),
        ],
        out_specs=(
            pl.BlockSpec(memory_space=pl.ANY),
            pl.BlockSpec(memory_space=pl.ANY),
            pl.BlockSpec(memory_space=pltpu.SMEM),
        ),
        scratch_shapes=[
            plane(pair, depth + 6), plane(depth + 6), plane(pair, depth + 4),
            plane(depth + 6), plane(depth + 6), plane(depth + 6), plane(depth + 6),
            plane(depth), plane(depth), plane(pair, depth), plane(pair, depth),
            pltpu.VMEM((2, 8, wy), f32), pltpu.VMEM((2, 8, wy), f32), pltpu.VMEM((slabs - 1, 2, 8, wy), f32),
            block(cross), block(cross), block(passes), block(passes), block(passes), block(passes),
            dma((2,)), dma((2, 4)), dma((6,)), dma((6,)),
            dma((chunks,)), dma((chunks,)), dma((chunks,)), dma((chunks,)), dma((chunks,)), dma((chunks,)),
            dma((slabs - 1,)), dma((slabs - 1,)),
        ],
        compiler_params=pltpu.CompilerParams(
            collective_id=passes + (0 if y_first else ROWS), has_side_effects=True, vmem_limit_bytes=56 * 2**20),
    )(parent, replica_field, momentum)


def routed(replica_field, momentum, parent):
    slabs = lax.axis_size("slab")
    plans = ((1, True, 5), (1, False, 5), (2, True, 3), (3, True, 2))
    branches = [functools.partial(run, passes, y_first, slabs, delay) for passes, y_first, delay in plans]
    return lax.switch(plan_for(parent), branches, replica_field, momentum, parent)


def padded(shard, sides, width):
    for axis, dim in sides:
        devices, length = (lax.axis_size(axis), shard.shape[dim])
        up = [(i, (i + 1) % devices) for i in range(devices)]
        down = [(j, i) for i, j in up]
        last = lax.slice_in_dim(shard, length - width, length, axis=dim)
        initial = lax.slice_in_dim(shard, 0, width, axis=dim)
        before = lax.ppermute(last, axis, up)
        after = lax.ppermute(initial, axis, down)
        shard = jnp.concatenate([before, shard, after], axis=dim)
    return shard


def force_inner(extended):
    center = extended[:, 1:-1]
    nearby = extended[:, :-2] + extended[:, 2:]
    nearby = nearby + jnp.roll(center, 1, 2) + jnp.roll(center, -1, 2)
    nearby = nearby + jnp.roll(center, 1, 3) + jnp.roll(center, -1, 3)
    return nearby - 6.0 * center - mass_square * center - coupling * center * center * center


def action_inner(extended):
    center = extended[:, 1:-1]
    along_z = extended[:, 2:] - center
    along_x = jnp.roll(center, -1, 2) - center
    along_y = jnp.roll(center, -1, 3) - center
    local = 0.5 * (along_z * along_z + along_x * along_x + along_y * along_y)
    local = (
        local
        + 0.5 * mass_square * center * center
        + 0.25 * coupling * center * center * center * center
    )
    return jnp.sum(local, axis=(1, 2, 3))


def extend_one(values):
    return padded(values, (("slab", 1),), 1)


def shards(replica_field, momentum, parent):
    per_group = replica_field.shape[0]
    depth = replica_field.shape[1]
    width_x = replica_field.shape[2]
    width_y = replica_field.shape[3]
    flat = replica_field.reshape(per_group, depth, width_x * width_y)
    spread = lax.all_to_all(flat, "rep", split_axis=2, concat_axis=0, tiled=True)
    copied = jnp.take(spread, parent, axis=0)
    returned = lax.all_to_all(copied, "rep", split_axis=0, concat_axis=2, tiled=True)
    field_start = returned.reshape(per_group, depth, width_x, width_y)
    volume = depth * lax.axis_size("slab") * width_x * width_y
    extended = extend_one(field_start)
    partial_action = action_inner(extended)
    half_kick = momentum + 0.5 * step_size * force_inner(extended)
    field_mid = field_start + step_size * half_kick
    kicked = half_kick + step_size * force_inner(extend_one(field_mid))
    field_end = field_mid + step_size * kicked
    momentum_end = kicked + 0.5 * step_size * force_inner(extend_one(field_end))
    density = lax.psum(partial_action, "slab") / volume
    return (field_end, momentum_end, density)


def solution(mesh):
    in_specs = (P("rep", "slab", None, None), P("rep", "slab", None, None), P())
    out_specs = (P("rep", "slab", None, None), P("rep", "slab", None, None), P("rep"))
    plan = routed if mesh.shape["rep"] == 2 * ROWS and mesh.shape["slab"] > 2 else shards
    return jax.shard_map(plan, mesh=mesh, in_specs=in_specs, out_specs=out_specs, check_vma=False)
```
